32 devices in a mesh: img: 4 (over y, core), tile: 8 (over z, x).
Axes of the slice: x: 2, y: 2, z: 4, core: 2. Of those that a mesh axis runs over, the one named last changes fastest.
Arguments:
- coarse: bfloat16 [4, 64, 8, 128], P('img', None, 'tile'), may hold values from -6 to 6
- w_first: bfloat16 [3, 3, 64, 32], replicated, may hold values from -0.25 to 0.25
- b_first: float32 [32], replicated, may hold values from -3 to 3
- w_second: bfloat16 [3, 3, 32, 32], replicated, may hold values from -0.375 to 0.375
- w_skip: bfloat16 [64, 32], replicated, may hold values from -0.75 to 0.75
- fade_alpha: float32 [1], replicated, may hold values from 0.3 to 0.7
- cotangent: bfloat16 [4, 32, 256, 16], P('img', None, 'tile'), may hold values from -6 to 6
Outputs:
- blended: bfloat16 [4, 32, 256, 16], P('img', None, 'tile')
- grad_first: float32 [3, 3, 64, 32], replicated
- grad_bias: float32 [32], replicated
- grad_second: float32 [3, 3, 32, 32], replicated
- grad_skip: float32 [64, 32], replicated
The draws below stay inside these ranges and needn't reach their ends.
All inputs are finite; a program needn't handle non-finite values.
Results may differ from the reference program's by a relative error of at most 0.0065.
Values may be sent and summed in bfloat16 or wider, within the bound.
No kernel may reach another device: no remote copies, remote signals or barrier semaphores. Data moves between devices by JAX's collectives and lax.ppermute only.
A program may use at most 64 MiB of HBM per device.

```python
import jax
import jax.numpy as jnp
from jax import lax

CIN = 64
COUT = 32
IMGS = 4
HC = 8
WC = 128
H = 16
W = 256


def block_scale(own_key, dims, split, least, high):
    factor_of = 1.0
    for axis_at, blocks in split:
        heights = jax.random.uniform(jax.random.fold_in(jax.random.fold_in(own_key, 6), axis_at), (blocks,), jnp.float32, least / len(split), high / len(split))
        factor_of = factor_of * jnp.repeat(jnp.exp(heights), dims[axis_at] // blocks).reshape((-1,) + (1,) * (len(dims) - 1 - axis_at))
    return factor_of


def scatter_about(own_key, dims, width, bound, split=(), kind=jnp.bfloat16):
    array = width * jax.random.normal(own_key, dims, jnp.float32)
    if split:
        array = array * block_scale(own_key, dims, split, -0.22, 0.18)
    return jnp.clip(array, -bound, bound).astype(kind)


def setup_inputs(seed: int = 0) -> dict:
    keys = jax.random.split(jax.random.key(seed), 8)
    coarse = scatter_about(keys[0], (IMGS, CIN, HC, WC), 1.0, 6.0, ((0, 4), (2, 8)))
    w_first = scatter_about(keys[1], (3, 3, CIN, COUT), (9 * CIN) ** -0.5, 0.25)
    b_first = scatter_about(keys[2], (COUT,), 0.5, 3.0, (), jnp.float32)
    w_second = scatter_about(keys[3], (3, 3, COUT, COUT), (9 * COUT) ** -0.5, 0.375)
    w_skip = scatter_about(keys[4], (CIN, COUT), CIN ** -0.5, 0.75)
    fade_alpha = jnp.clip(jax.random.uniform(keys[5], (1,), jnp.float32, 0.3, 0.7), 0.3, 0.7)
    cotangent = scatter_about(keys[6], (IMGS, COUT, W, H), 1.0, 6.0, ((0, 4), (2, 8)))
    return dict(coarse=coarse, w_first=w_first, b_first=b_first, w_second=w_second, w_skip=w_skip, fade_alpha=fade_alpha, cotangent=cotangent)


def upsample_axis(values, low_rim, high_rim, along):
    length = values.shape[along]
    left_side = jnp.concatenate([low_rim, lax.slice_in_dim(values, 0, length - 1, axis=along)], along)
    right_side = jnp.concatenate([lax.slice_in_dim(values, 1, length, axis=along), high_rim], along)
    even_part = 0.25 * left_side + 0.75 * values
    odd_part = 0.75 * values + 0.25 * right_side
    stacked = jnp.stack([even_part, odd_part], along + 1)
    new_shape = list(values.shape)
    new_shape[along] = 2 * length
    return stacked.reshape(new_shape)


def conv_shift(padded, kernel, out_width, height):
    summed = None
    for shift_w in range(3):
        for shift_h in range(3):
            window_part = padded[:, :, shift_w:shift_w + out_width, shift_h:shift_h + height].astype(jnp.float32)
            term = jnp.einsum("bcwh,co->bowh", window_part, kernel[shift_w, shift_h].astype(jnp.float32))
            summed = term if summed is None else summed + term
    return summed


def conv_adjoint(padded, kernel, out_width, height):
    summed = None
    for shift_w in range(3):
        for shift_h in range(3):
            window_part = padded[:, :, 2 - shift_w:2 - shift_w + out_width, 2 - shift_h:2 - shift_h + height].astype(jnp.float32)
            term = jnp.einsum("bowh,co->bcwh", window_part, kernel[shift_w, shift_h].astype(jnp.float32))
            summed = term if summed is None else summed + term
    return summed


def weight_terms(padded, delta, out_width, height):
    outer_list = []
    for shift_w in range(3):
        inner_list = []
        for shift_h in range(3):
            window_part = padded[:, :, shift_w:shift_w + out_width, shift_h:shift_h + height].astype(jnp.float32)
            inner_list.append(jnp.einsum("bcwh,bowh->co", window_part, delta.astype(jnp.float32)))
        outer_list.append(jnp.stack(inner_list))
    return jnp.stack(outer_list)


def pad_plane(values):
    return jnp.pad(values, ((0, 0), (0, 0), (1, 1), (1, 1)))


def reference(coarse, w_first, b_first, w_second, w_skip, fade_alpha, cotangent):
    blend = fade_alpha[0]
    loss_scale = float(IMGS * W * H) ** -0.5

    def one_image(image_pair):
        features, grad_image = image_pair
        values = features[None].astype(jnp.float32)
        row_pass = upsample_axis(values, values[:, :, :1], values[:, :, -1:], 2)
        col_pass = upsample_axis(row_pass, row_pass[:, :, :, :1], row_pass[:, :, :, -1:], 3)
        upsampled = jnp.transpose(col_pass, (0, 1, 3, 2)).astype(jnp.bfloat16)
        up_pad = pad_plane(upsampled)
        pre_first = conv_shift(up_pad, w_first, W, H) + b_first[None, :, None, None]
        hidden = jax.nn.silu(pre_first).astype(jnp.bfloat16)
        hidden_pad = pad_plane(hidden)
        second_out = conv_shift(hidden_pad, w_second, W, H)
        skip_out = jnp.einsum("bcwh,co->bowh", upsampled.astype(jnp.float32), w_skip.astype(jnp.float32))
        blended = (blend * second_out + (1.0 - blend) * skip_out).astype(jnp.bfloat16)
        grad_float = grad_image[None].astype(jnp.float32)
        d_second = (grad_float * (blend * loss_scale)).astype(jnp.bfloat16)
        d_skip = (grad_float * ((1.0 - blend) * loss_scale)).astype(jnp.bfloat16)
        d_hidden = conv_adjoint(pad_plane(d_second), w_second, W, H)
        sigma = jax.nn.sigmoid(pre_first)
        d_pre = (d_hidden * (sigma * (1.0 + pre_first * (1.0 - sigma)))).astype(jnp.bfloat16)
        grad_first = weight_terms(up_pad, d_pre, W, H)
        grad_bias = jnp.sum(d_pre.astype(jnp.float32), axis=(0, 2, 3))
        grad_second = weight_terms(hidden_pad, d_second, W, H)
        grad_skip = jnp.einsum("bcwh,bowh->co", upsampled.astype(jnp.float32), d_skip.astype(jnp.float32))
        return blended[0], grad_first, grad_bias, grad_second, grad_skip

    blended, grad_first, grad_bias, grad_second, grad_skip = lax.map(one_image, (coarse, cotangent))
    return (blended, jnp.sum(grad_first, axis=0), jnp.sum(grad_bias, axis=0),
            jnp.sum(grad_second, axis=0), jnp.sum(grad_skip, axis=0))
```

```python
import functools
import math

import jax
import jax.numpy as jnp
from jax import lax
from jax.experimental import pallas as pl
from jax.experimental.pallas import tpu as pltpu
from jax.sharding import PartitionSpec as P

F32 = jnp.float32
BF16 = jnp.bfloat16
ROWS = 16
NT = (((1,), (1,)), ((), ()))


def up128(n):
    return -(-n // 128) * 128


def ints(shape, dim):
    return lax.broadcasted_iota(jnp.int32, shape, dim)


def quotient(values, divisor):
    return ((values.astype(F32) + 0.5) * (1.0 / divisor)).astype(jnp.int32)


class Sizes:
    def __init__(self, coarse, cotangent, tiles):
        self.tiles = tiles
        self.cin = coarse.shape[1]
        self.cout = cotangent.shape[1]
        self.coarse_rows = coarse.shape[2] * tiles
        self.coarse_cols = coarse.shape[3]
        self.own_coarse = self.coarse_cols // tiles
        self.width = cotangent.shape[2]
        self.height = cotangent.shape[3]
        self.pitch = self.width + 4
        self.window = self.own_coarse + 4
        self.half = self.window // 2
        self.lanes = up128(self.height * self.pitch)
        self.wide = up128(self.lanes + 2 * self.pitch + 2)


def pack_kernel(z, coarse_ref, out_ref):
    row = coarse_ref[...]
    count = z.tiles * ROWS
    at = ints((count, z.coarse_cols), 0)
    col = ints((count, z.coarse_cols), 1)
    dest = lax.shift_right_logical(at, 4)
    slot = lax.bitwise_and(at, ROWS - 1)
    parts = []
    for half in range(2):
        want = dest * z.own_coarse - 2 + half * z.half + slot
        want = jnp.clip(want, 0, z.coarse_cols - 1)
        pick = jnp.where((want == col) & (slot < z.half), 1.0, 0.0).astype(BF16)
        parts.append(lax.dot_general(pick, row, NT, preferred_element_type=F32))
    packed = jnp.concatenate(parts, axis=1).astype(BF16)
    out_ref[...] = packed.reshape(out_ref.shape)


def prepare_kernel(
    z, scale, cot_ref, wf_ref, ws_ref, alpha_ref, d_hidden_ref, spread_ref, dskip_ref, wf_cat_ref,
    tall_ref, flat_ref,
):
    blend = alpha_ref[0]
    tall_ref[:, : z.width] = cot_ref[...].astype(F32).reshape(z.cout * z.height, z.width)
    flat_ref[...] = jnp.zeros(flat_ref.shape, F32)
    for h in range(z.height):
        piece = tall_ref[pl.ds(h, z.cout, stride=z.height), :]
        start = (h + 1) * z.pitch + 3
        flat_ref[:, start : start + z.width] = piece[:, : z.width]
    flat = flat_ref[...]
    d_second = (flat * (blend * scale)).astype(BF16).astype(F32)
    centre = z.pitch + 1
    dskip_ref[...] = pltpu.roll(flat * ((1.0 - blend) * scale), z.wide - centre, 1)[
        :, : z.lanes
    ].astype(BF16)
    back = []
    for p in range(3):
        for q in range(3):
            start = (2 - q) * z.pitch + 2 - p
            moved = d_second if start == 0 else pltpu.roll(d_second, z.wide - start, 1)
            k = (p * 3 + q) * z.cout
            spread_ref[k : k + z.cout, :] = moved[:, : z.lanes].astype(BF16)
            back.append(ws_ref[p, q])
            c = (p * 3 + q) * z.cin
            wf_cat_ref[:, c : c + z.cin] = wf_ref[p, q]
    d_hidden_ref[...] = jnp.dot(
        jnp.concatenate(back, axis=1), spread_ref[...], preferred_element_type=F32
    )


def main_kernel(
    z, got_ref, d_hidden_ref, spread_ref, dskip_ref, wf_cat_ref, bias_ref,
    grads_ref, up_ref, hidden_ref, interp_ref, taps_ref,
):
    position = lax.axis_index("tile")
    n = ints((ROWS, z.wide), 1) - 1
    slot = ints((ROWS, z.wide), 0)
    h = quotient(n + z.pitch, z.pitch) - 2
    w = n - (h + 1) * z.pitch
    column = position * z.width + w - 2
    inside = (h >= 0) & (h < z.height) & (column >= 0) & (column < z.width * z.tiles)
    w_main = lax.shift_right_logical(w, 1) + 1
    w_other = w_main - 1 + 2 * lax.bitwise_and(w, 1)
    h_main = lax.shift_right_arithmetic(h, 1)
    h_other = jnp.clip(h_main - 1 + 2 * lax.bitwise_and(h, 1), 0, z.coarse_rows - 1)
    col_weights = []
    for half in range(2):
        at = slot + half * z.half
        weight = jnp.where(at == w_main, 0.75, 0.0) + jnp.where(at == w_other, 0.25, 0.0)
        col_weights.append(jnp.where(inside & (slot < z.half), weight, 0.0))
    span = z.coarse_rows * ROWS

    def one_row(r, carry):
        weight = jnp.where(h_main == r, 0.75, 0.0) + jnp.where(h_other == r, 0.25, 0.0)
        for half in range(2):
            at = pl.multiple_of(half * span + r * ROWS, ROWS)
            interp_ref[pl.ds(at, ROWS), :] = (col_weights[half] * weight).astype(BF16)
        return carry

    lax.fori_loop(0, z.coarse_rows, one_row, 0, unroll=z.coarse_rows <= 8)

    turned = got_ref[...].reshape(span, 2 * z.cin).T
    both = jnp.concatenate([turned[: z.cin], turned[z.cin :]], axis=1)
    up = jnp.dot(both, interp_ref[...], preferred_element_type=F32).astype(BF16)
    up32 = up.astype(F32)
    for p in range(3):
        for q in range(3):
            start = q * z.pitch + p
            moved = up32 if start == 0 else pltpu.roll(up32, z.wide - start, 1)
            k = (p * 3 + q) * z.cin
            taps_ref[k : k + z.cin, :] = moved[:, : z.lanes].astype(BF16)
    taps = taps_ref[...]
    centre = taps_ref[4 * z.cin : 5 * z.cin, :]
    up_ref[...] = centre
    pre = jnp.dot(wf_cat_ref[...], taps, preferred_element_type=F32) + bias_ref[...]
    sigma = 1.0 / (1.0 + jnp.exp(-pre))
    m = ints((z.cout, z.lanes), 1)
    mh = quotient(m, z.pitch)
    mw = m - mh * z.pitch
    column = position * z.width + mw - 2
    inside = (mw >= 1) & (mw <= z.width + 2) & (mh < z.height)
    inside = inside & (column >= 0) & (column < z.width * z.tiles)
    hidden = jnp.where(inside, pre * sigma, 0.0).astype(BF16)
    hidden_ref[...] = hidden
    slope = sigma * (1.0 + pre * (1.0 - sigma))
    d_pre = jnp.where(inside, d_hidden_ref[...] * slope, 0.0).astype(BF16)
    first = lax.dot_general(d_pre, taps, NT, preferred_element_type=F32)
    second = lax.dot_general(hidden, spread_ref[...], NT, preferred_element_type=F32)
    skip = lax.dot_general(dskip_ref[...], centre, NT, preferred_element_type=F32)
    ones = jnp.ones((z.cout, z.lanes), BF16)
    biases = lax.dot_general(ones, d_pre, NT, preferred_element_type=F32)
    full = grads_ref.shape[1]
    used = 9 * z.cin + 9 * z.cout + z.cin + z.cout
    pieces = [first, second, skip, biases]
    if full > used:
        pieces.append(jnp.zeros((z.cout, full - used), F32))
    grads_ref[...] = jnp.concatenate(pieces, axis=1).astype(BF16)


def blend_kernel(z, hidden_ref, up_ref, ws_ref, wk_ref, alpha_ref, out_ref, tall_ref):
    blend = alpha_ref[0]
    padded = jnp.concatenate(
        [hidden_ref[...].astype(F32), jnp.zeros((z.cout, z.wide - z.lanes), F32)], axis=1
    )
    padded = pltpu.roll(padded, z.pitch + 1, 1)
    taps = []
    for p in range(3):
        for q in range(3):
            start = q * z.pitch + p
            moved = padded if start == 0 else pltpu.roll(padded, z.wide - start, 1)
            taps.append(moved[:, : z.lanes].astype(BF16))
    taps = jnp.concatenate(taps, axis=0)
    kernel = ws_ref[...].reshape(9 * z.cout, z.cout).T
    second = jnp.dot(kernel, taps, preferred_element_type=F32)
    skip = jnp.dot(wk_ref[...], up_ref[...], preferred_element_type=F32)
    mixed = blend * second + (1.0 - blend) * skip
    for h in range(z.height):
        start = h * z.pitch + 2
        tall_ref[pl.ds(h, z.cout, stride=z.height), : z.width] = mixed[:, start : start + z.width]
    out_ref[...] = tall_ref[:, : z.width].reshape(out_ref.shape).astype(BF16)


def finish_kernel(z, mine_ref, other_ref, first_ref, bias_ref, second_ref, skip_ref):
    total = mine_ref[...].astype(F32) + other_ref[...].astype(F32)
    at = 0
    for p in range(3):
        for q in range(3):
            first_ref[p, q] = total[:, at : at + z.cin]
            at += z.cin
    for p in range(3):
        for q in range(3):
            second_ref[p, q] = total[:, at : at + z.cout]
            at += z.cout
    skip_ref[...] = total[:, at : at + z.cin]
    at += z.cin
    bias_ref[...] = total[0:1, at : at + z.cout]


def call(body, outs, specs, scratch=(), flops=1000000):
    return pl.pallas_call(
        body,
        out_shape=outs,
        in_specs=specs,
        out_specs=jax.tree.map(lambda _: pl.BlockSpec(memory_space=pltpu.VMEM), outs),
        scratch_shapes=scratch,
        compiler_params=pltpu.CompilerParams(vmem_limit_bytes=48 * 1024 * 1024),
        cost_estimate=pl.CostEstimate(flops=flops, bytes_accessed=200000, transcendentals=0),
    )


def butterfly(images, tiles):
    steps = []
    side = 1 if images % 2 == 0 else 0
    k = 1
    while k < images:
        steps.append((k | side if k > 1 else k, 0))
        k *= 2
    k = 1
    while k < tiles:
        steps.append((side, k))
        k *= 2
    return [
        [(i * tiles + t, (i ^ a) * tiles + (t ^ b)) for i in range(images) for t in range(tiles)]
        for a, b in steps
    ]


def local(coarse, w_first, b_first, w_second, w_skip, fade_alpha, cotangent):
    tiles = lax.axis_size("tile")
    images = lax.axis_size("img")
    z = Sizes(coarse, cotangent, tiles)
    vmem = pl.BlockSpec(memory_space=pltpu.VMEM)
    smem = pl.BlockSpec(memory_space=pltpu.SMEM)
    bf, f32 = (lambda *s: jax.ShapeDtypeStruct(s, BF16)), (lambda *s: jax.ShapeDtypeStruct(s, F32))
    total_count = coarse.shape[0] * images * z.width * tiles * z.height
    scale = float(total_count) ** (-0.5)

    packed = call(
        functools.partial(pack_kernel, z), bf(tiles, ROWS, 2 * z.cin), [vmem]
    )(coarse.reshape(z.cin, z.coarse_cols))
    got = lax.all_to_all(packed, "tile", split_axis=0, concat_axis=0, tiled=True)

    cot = jnp.transpose(cotangent[0], (0, 2, 1))
    wf = jnp.transpose(w_first, (0, 1, 3, 2))
    d_hidden, spread, dskip, wf_cat = call(
        functools.partial(prepare_kernel, z, scale),
        (f32(z.cout, z.lanes), bf(9 * z.cout, z.lanes), bf(z.cout, z.lanes), bf(z.cout, 9 * z.cin)),
        [vmem, vmem, vmem, smem],
        [pltpu.VMEM((z.cout * z.height, 128), F32), pltpu.VMEM((z.cout, z.wide), F32)],
    )(cot, wf, w_second, fade_alpha)

    columns = up128(10 * z.cin + 10 * z.cout)
    grads, up, hidden = call(
        functools.partial(main_kernel, z),
        (bf(z.cout, columns), bf(z.cin, z.lanes), bf(z.cout, z.lanes)),
        [vmem] * 6,
        [
            pltpu.VMEM((2 * z.coarse_rows * ROWS, z.wide), BF16),
            pltpu.VMEM((9 * z.cin, z.lanes), BF16),
        ],
    )(got, d_hidden, spread, dskip, wf_cat, b_first.reshape(z.cout, 1))

    blended = call(
        functools.partial(blend_kernel, z),
        bf(z.cout, z.height, z.width),
        [vmem, vmem, vmem, vmem, smem],
        [pltpu.VMEM((z.cout * z.height, 128), F32)],
    )(hidden, up, w_second, jnp.transpose(w_skip), fade_alpha)

    steps = butterfly(images, tiles)
    for pairs in steps[:-1]:
        other = lax.ppermute(grads, ("img", "tile"), pairs)
        grads = (grads.astype(F32) + other.astype(F32)).astype(BF16)
    other = lax.ppermute(grads, ("img", "tile"), steps[-1])
    first, bias, second, skip = call(
        functools.partial(finish_kernel, z),
        (f32(3, 3, z.cout, z.cin), f32(1, z.cout), f32(3, 3, z.cout, z.cout), f32(z.cout, z.cin)),
        [vmem, vmem],
    )(grads, other)
    return (
        jnp.transpose(blended, (0, 2, 1))[None],
        jnp.transpose(first, (0, 1, 3, 2)),
        bias.reshape(z.cout),
        second,
        jnp.transpose(skip),
    )


def solution(mesh):
    placed = (P("img", None, "tile", None), P(), P(), P(), P(), P(), P("img", None, "tile", None))
    return jax.shard_map(
        local,
        mesh=mesh,
        in_specs=placed,
        out_specs=(P("img", None, "tile", None), P(), P(), P(), P()),
        check_vma=False,
    )
```

```python
import functools

import jax
import jax.numpy as jnp
from jax import lax
from jax.experimental import pallas as pl
from jax.experimental.pallas import tpu as pltpu
from jax.sharding import PartitionSpec as P

F32 = jnp.float32
BF16 = jnp.bfloat16
ROWS = 16
NT = (((1,), (1,)), ((), ()))


def up128(n):
    return -(-n // 128) * 128


def ints(shape, dim):
    return lax.broadcasted_iota(jnp.int32, shape, dim)


def quotient(values, divisor):
    return ((values.astype(F32) + 0.5) * (1.0 / divisor)).astype(jnp.int32)


class Sizes:
    def __init__(self, coarse, cotangent, images, tiles):
        self.images = images
        self.tiles = tiles
        self.cin = coarse.shape[1]
        self.cout = cotangent.shape[1]
        self.coarse_rows = coarse.shape[2] * tiles
        self.coarse_cols = coarse.shape[3]
        self.own_coarse = self.coarse_cols // tiles
        self.width = cotangent.shape[2]
        self.height = cotangent.shape[3]
        self.pitch = self.width + 4
        self.window = self.own_coarse + 4
        self.half = self.window // 2
        self.lanes = up128(self.height * self.pitch)
        self.wide = up128(self.lanes + 2 * self.pitch + 2)


def pack_kernel(z, coarse_ref, out_ref):
    row = coarse_ref[...]
    count = z.tiles * ROWS
    at = ints((count, z.coarse_cols), 0)
    col = ints((count, z.coarse_cols), 1)
    dest = lax.shift_right_logical(at, 4)
    slot = lax.bitwise_and(at, ROWS - 1)
    parts = []
    for half in range(2):
        want = dest * z.own_coarse - 2 + half * z.half + slot
        want = jnp.clip(want, 0, z.coarse_cols - 1)
        pick = jnp.where((want == col) & (slot < z.half), 1.0, 0.0).astype(BF16)
        parts.append(lax.dot_general(pick, row, NT, preferred_element_type=F32))
    packed = jnp.concatenate(parts, axis=1).astype(BF16)
    out_ref[...] = packed.reshape(out_ref.shape)


def interpolation(z, position, interp_ref):
    n = ints((ROWS, z.wide), 1) - 1
    slot = ints((ROWS, z.wide), 0)
    h = quotient(n + z.pitch, z.pitch) - 2
    w = n - (h + 1) * z.pitch
    column = position * z.width + w - 2
    inside = (h >= 0) & (h < z.height) & (column >= 0) & (column < z.width * z.tiles)
    w_main = lax.shift_right_logical(w, 1) + 1
    w_other = w_main - 1 + 2 * lax.bitwise_and(w, 1)
    h_main = lax.shift_right_arithmetic(h, 1)
    h_other = jnp.clip(h_main - 1 + 2 * lax.bitwise_and(h, 1), 0, z.coarse_rows - 1)
    col_weights = []
    for half in range(2):
        at = slot + half * z.half
        weight = jnp.where(at == w_main, 0.75, 0.0) + jnp.where(at == w_other, 0.25, 0.0)
        col_weights.append(jnp.where(inside & (slot < z.half), weight, 0.0))
    span = z.coarse_rows * ROWS

    def one_row(r, carry):
        weight = jnp.where(h_main == r, 0.75, 0.0) + jnp.where(h_other == r, 0.25, 0.0)
        for half in range(2):
            at = pl.multiple_of(half * span + r * ROWS, ROWS)
            interp_ref[pl.ds(at, ROWS), :] = (col_weights[half] * weight).astype(BF16)
        return carry

    lax.fori_loop(0, z.coarse_rows, one_row, 0, unroll=z.coarse_rows <= 8)


def prepare_kernel(
    z, scale, cot_ref, ws_ref, row_ref, d_hidden_ref, spread_ref, dskip_ref, interp_ref, bias_ref,
    tall_ref, flat_ref,
):
    blend = row_ref[:, z.cout :]
    interpolation(z, lax.axis_index("tile"), interp_ref)
    diagonal = ints((z.cout, z.cout), 0) == ints((z.cout, z.cout), 1)
    bias_ref[...] = jnp.sum(jnp.where(diagonal, row_ref[:, : z.cout], 0.0), axis=1, keepdims=True)
    flat_ref[...] = jnp.zeros(flat_ref.shape, F32)
    tall_ref[:, : z.width] = cot_ref[...].astype(F32).reshape(z.cout * z.height, z.width)
    for h in range(z.height):
        piece = tall_ref[pl.ds(h, z.cout, stride=z.height), :]
        start = (h + 1) * z.pitch + 3
        flat_ref[:, start : start + z.width] = piece[:, : z.width]
    flat = flat_ref[...]
    d_second = (flat * (blend * scale)).astype(BF16).astype(F32)
    dskip_ref[...] = pltpu.roll(flat * ((1.0 - blend) * scale), z.wide - (z.pitch + 1), 1)[
        :, : z.lanes
    ].astype(BF16)
    back = []
    for p in range(3):
        for q in range(3):
            start = (2 - q) * z.pitch + 2 - p
            moved = d_second if start == 0 else pltpu.roll(d_second, z.wide - start, 1)
            k = (p * 3 + q) * z.cout
            spread_ref[k : k + z.cout, :] = moved[:, : z.lanes].astype(BF16)
            back.append(ws_ref[p, q])
    d_hidden_ref[...] = jnp.dot(
        jnp.concatenate(back, axis=1), spread_ref[...], preferred_element_type=F32
    )


def holds_top(z):
    image, tile = lax.axis_index("img"), lax.axis_index("tile")
    bits = jnp.int32(0)
    for index, count in ((image, z.images), (tile, z.tiles)):
        k = 1
        while k < count:
            bits = bits ^ (lax.div(index, jnp.int32(k)) & 1)
            k *= 2
    return bits == 0


def main_kernel(
    z, got_ref, d_hidden_ref, spread_ref, dskip_ref, wf_ref, bias_ref, interp_ref,
    keep_ref, give_ref, up_ref, hidden_ref, taps_ref,
):
    position = lax.axis_index("tile")
    turned = got_ref[...].reshape(z.coarse_rows * ROWS, 2 * z.cin).T
    both = jnp.concatenate([turned[: z.cin], turned[z.cin :]], axis=1)
    up = jnp.dot(both, interp_ref[...], preferred_element_type=F32).astype(BF16)
    up32 = up.astype(F32)
    for p in range(3):
        for q in range(3):
            start = q * z.pitch + p
            moved = up32 if start == 0 else pltpu.roll(up32, z.wide - start, 1)
            k = (p * 3 + q) * z.cin
            taps_ref[k : k + z.cin, :] = moved[:, : z.lanes].astype(BF16)
    taps = taps_ref[...]
    centre = taps_ref[4 * z.cin : 5 * z.cin, :]
    up_ref[...] = centre
    kernel = jnp.concatenate([wf_ref[p, q] for p in range(3) for q in range(3)], axis=1)
    pre = jnp.dot(kernel, taps, preferred_element_type=F32) + bias_ref[...]
    sigma = 1.0 / (1.0 + jnp.exp(-pre))
    m = ints((z.cout, z.lanes), 1)
    mh = quotient(m, z.pitch)
    mw = m - mh * z.pitch
    column = position * z.width + mw - 2
    inside = (mw >= 1) & (mw <= z.width + 2) & (mh < z.height)
    inside = inside & (column >= 0) & (column < z.width * z.tiles)
    hidden = jnp.where(inside, pre * sigma, 0.0).astype(BF16)
    hidden_ref[...] = hidden
    slope = sigma * (1.0 + pre * (1.0 - sigma))
    d_pre = jnp.where(inside, d_hidden_ref[...] * slope, 0.0).astype(BF16)
    first = lax.dot_general(d_pre, taps, NT, preferred_element_type=F32)
    second = lax.dot_general(hidden, spread_ref[...], NT, preferred_element_type=F32)
    skip = lax.dot_general(dskip_ref[...], centre, NT, preferred_element_type=F32)
    ones = jnp.ones((z.cout, z.lanes), BF16)
    biases = lax.dot_general(ones, d_pre, NT, preferred_element_type=F32)
    full = keep_ref.shape[1]
    used = 10 * z.cin + 10 * z.cout
    pieces = [first, second, skip, biases]
    if full > used:
        pieces.append(jnp.zeros((z.cout, full - used), F32))
    grads = jnp.concatenate(pieces, axis=1)
    half = z.cout // 2
    top = holds_top(z)
    keep_ref[...] = jnp.where(top, grads[:half], grads[half:])
    give_ref[...] = jnp.where(top, grads[half:], grads[:half])


def blend_kernel(z, hidden_ref, up_ref, ws_ref, wk_ref, row_ref, out_ref, tall_ref):
    blend = row_ref[:, z.cout :]
    padded = jnp.concatenate(
        [hidden_ref[...].astype(F32), jnp.zeros((z.cout, z.wide - z.lanes), F32)], axis=1
    )
    padded = pltpu.roll(padded, z.pitch + 1, 1)
    taps = []
    for p in range(3):
        for q in range(3):
            start = q * z.pitch + p
            moved = padded if start == 0 else pltpu.roll(padded, z.wide - start, 1)
            taps.append(moved[:, : z.lanes].astype(BF16))
    taps = jnp.concatenate(taps, axis=0)
    kernel = ws_ref[...].reshape(9 * z.cout, z.cout).T
    second = jnp.dot(kernel, taps, preferred_element_type=F32)
    skip = jnp.dot(wk_ref[...], up_ref[...], preferred_element_type=F32)
    mixed = blend * second + (1.0 - blend) * skip
    for h in range(z.height):
        start = h * z.pitch + 2
        tall_ref[pl.ds(h, z.cout, stride=z.height), : z.width] = mixed[:, start : start + z.width]
    out_ref[...] = tall_ref[:, : z.width].reshape(out_ref.shape).astype(BF16)


def finish_kernel(z, mine_ref, other_ref, first_ref, bias_ref, second_ref, skip_ref):
    top = holds_top(z)
    mine, other = mine_ref[...], other_ref[...]
    total = jnp.concatenate(
        [jnp.where(top, mine, other), jnp.where(top, other, mine)], axis=0
    )
    at = 0
    for p in range(3):
        for q in range(3):
            first_ref[p, q] = total[:, at : at + z.cin]
            at += z.cin
    for p in range(3):
        for q in range(3):
            second_ref[p, q] = total[:, at : at + z.cout]
            at += z.cout
    skip_ref[...] = total[:, at : at + z.cin]
    at += z.cin
    bias_ref[...] = total[0:1, at : at + z.cout]


def call(body, outs, specs, scratch=(), flops=1000000):
    return pl.pallas_call(
        body,
        out_shape=outs,
        in_specs=specs,
        out_specs=jax.tree.map(lambda _: pl.BlockSpec(memory_space=pltpu.VMEM), outs),
        scratch_shapes=scratch,
        compiler_params=pltpu.CompilerParams(vmem_limit_bytes=48 * 1024 * 1024),
        cost_estimate=pl.CostEstimate(flops=flops, bytes_accessed=200000, transcendentals=0),
    )


def swap(values, images, tiles, across):
    a, b = across
    pairs = [
        (i * tiles + t, (i ^ a) * tiles + (t ^ b)) for i in range(images) for t in range(tiles)
    ]
    return lax.ppermute(values, ("img", "tile"), pairs)


def total_over_chips(mine, images, tiles):
    bits = []
    k = 2
    while k < images:
        bits.append((k, 0))
        k *= 2
    k = 1
    while k < tiles:
        bits.append((0, k))
        k *= 2
    for at in range(0, len(bits), 2):
        group = bits[at : at + 2]
        sent = mine.astype(BF16)
        partners = [(a ^ 1, b) for a, b in group]
        if len(group) == 2:
            partners.append((group[0][0] ^ group[1][0], group[0][1] ^ group[1][1]))
        got = [swap(sent, images, tiles, across).astype(F32) for across in partners]
        mine = sent.astype(F32) + got[0]
        if len(got) == 3:
            mine = mine + (got[1] + got[2])
    return mine


def local(coarse, w_first, b_first, w_second, w_skip, fade_alpha, cotangent):
    tiles = lax.axis_size("tile")
    images = lax.axis_size("img")
    z = Sizes(coarse, cotangent, images, tiles)
    vmem = pl.BlockSpec(memory_space=pltpu.VMEM)
    bf, f32 = (lambda *s: jax.ShapeDtypeStruct(s, BF16)), (lambda *s: jax.ShapeDtypeStruct(s, F32))
    total_count = coarse.shape[0] * images * z.width * tiles * z.height
    scale = float(total_count) ** (-0.5)

    cot = jnp.transpose(cotangent[0], (0, 2, 1))
    wf = jnp.transpose(w_first, (0, 1, 3, 2))
    row = jnp.concatenate([b_first, fade_alpha]).reshape(1, z.cout + 1)
    packed = call(
        functools.partial(pack_kernel, z), bf(tiles, ROWS, 2 * z.cin), [vmem]
    )(coarse.reshape(z.cin, z.coarse_cols))
    got = lax.all_to_all(packed, "tile", split_axis=0, concat_axis=0, tiled=True)

    d_hidden, spread, dskip, interp, bias = call(
        functools.partial(prepare_kernel, z, scale),
        (
            f32(z.cout, z.lanes),
            bf(9 * z.cout, z.lanes),
            bf(z.cout, z.lanes),
            bf(2 * z.coarse_rows * ROWS, z.wide),
            f32(z.cout, 1),
        ),
        [vmem] * 3,
        [pltpu.VMEM((z.cout * z.height, 128), F32), pltpu.VMEM((z.cout, z.wide), F32)],
    )(cot, w_second, row)

    columns = up128(10 * z.cin + 10 * z.cout)
    half = z.cout // 2
    keep, give, up, hidden = call(
        functools.partial(main_kernel, z),
        (f32(half, columns), f32(half, columns), bf(z.cin, z.lanes), bf(z.cout, z.lanes)),
        [vmem] * 7,
        [pltpu.VMEM((9 * z.cin, z.lanes), BF16)],
    )(got, d_hidden, spread, dskip, wf, bias, interp)

    blended = call(
        functools.partial(blend_kernel, z),
        bf(z.cout, z.height, z.width),
        [vmem] * 5,
        [pltpu.VMEM((z.cout * z.height, 128), F32)],
    )(hidden, up, w_second, jnp.transpose(w_skip), row)

    mine = keep + swap(give, images, tiles, (1, 0))
    mine = total_over_chips(mine, images, tiles)
    mine, blended = lax.optimization_barrier((mine, blended))
    other = swap(mine, images, tiles, (1, 0))
    first, bias, second, skip = call(
        functools.partial(finish_kernel, z),
        (f32(3, 3, z.cout, z.cin), f32(1, z.cout), f32(3, 3, z.cout, z.cout), f32(z.cout, z.cin)),
        [vmem] * 2,
    )(mine, other)
    return (
        jnp.transpose(blended, (0, 2, 1))[None],
        jnp.transpose(first, (0, 1, 3, 2)),
        bias.reshape(z.cout),
        second,
        jnp.transpose(skip),
    )


def solution(mesh):
    placed = (P("img", None, "tile", None), P(), P(), P(), P(), P(), P("img", None, "tile", None))
    return jax.shard_map(
        local,
        mesh=mesh,
        in_specs=placed,
        out_specs=(P("img", None, "tile", None), P(), P(), P(), P()),
        check_vma=False,
    )
```

```python
import functools

import jax
import jax.numpy as jnp
from jax import lax
from jax.experimental import pallas as pl
from jax.experimental.pallas import tpu as pltpu
from jax.sharding import PartitionSpec as P

F32 = jnp.float32
BF16 = jnp.bfloat16
ROWS = 16
NT = (((1,), (1,)), ((), ()))


def up128(n):
    return -(-n // 128) * 128


def ints(shape, dim):
    return lax.broadcasted_iota(jnp.int32, shape, dim)


def quotient(values, divisor):
    return ((values.astype(F32) + 0.5) * (1.0 / divisor)).astype(jnp.int32)


class Sizes:
    def __init__(self, coarse, cotangent, images, tiles):
        self.images = images
        self.tiles = tiles
        self.cin = coarse.shape[1]
        self.cout = cotangent.shape[1]
        self.coarse_rows = coarse.shape[2] * tiles
        self.coarse_cols = coarse.shape[3]
        self.own_coarse = self.coarse_cols // tiles
        self.width = cotangent.shape[2]
        self.height = cotangent.shape[3]
        self.pitch = self.width + 4
        self.window = self.own_coarse + 4
        self.half = self.window // 2
        self.lanes = up128(self.height * self.pitch)
        self.pair = tiles // 2
        self.both = 2 * self.lanes
        self.wide = up128(self.lanes + 2 * self.pitch + 2)


def pack_kernel(z, coarse_ref, out_ref):
    row = coarse_ref[...]
    count = z.tiles * 2 * ROWS
    at = ints((count, z.coarse_cols), 0)
    col = ints((count, z.coarse_cols), 1)
    dest = lax.shift_right_logical(at, 5)
    strip = lax.bitwise_and(lax.shift_right_logical(at, 4), 1)
    tile = lax.bitwise_and(dest, z.pair - 1) + strip * z.pair
    slot = lax.bitwise_and(at, ROWS - 1)
    parts = []
    for half in range(2):
        want = tile * z.own_coarse - 2 + half * z.half + slot
        want = jnp.clip(want, 0, z.coarse_cols - 1)
        pick = jnp.where((want == col) & (slot < z.half), 1.0, 0.0).astype(BF16)
        parts.append(lax.dot_general(pick, row, NT, preferred_element_type=F32))
    packed = jnp.concatenate(parts, axis=1).astype(BF16)
    out_ref[...] = packed.reshape(out_ref.shape)


def strips(z):
    position = lax.axis_index("tile")
    low = lax.bitwise_and(position, z.pair - 1)
    return (low, low + z.pair), position < z.pair


def interpolation(z, interp_ref):
    n = ints((ROWS, z.wide), 1) - 1
    slot = ints((ROWS, z.wide), 0)
    h = quotient(n + z.pitch, z.pitch) - 2
    w = n - (h + 1) * z.pitch
    inside = (h >= 0) & (h < z.height)
    w_main = lax.shift_right_logical(w, 1) + 1
    w_other = w_main - 1 + 2 * lax.bitwise_and(w, 1)
    h_main = lax.shift_right_arithmetic(h, 1)
    h_other = jnp.clip(h_main - 1 + 2 * lax.bitwise_and(h, 1), 0, z.coarse_rows - 1)
    col_weights = []
    for half in range(2):
        at = slot + half * z.half
        weight = jnp.where(at == w_main, 0.75, 0.0) + jnp.where(at == w_other, 0.25, 0.0)
        col_weights.append(jnp.where(inside & (slot < z.half), weight, 0.0))
    span = z.coarse_rows * ROWS

    def one_row(r, carry):
        weight = jnp.where(h_main == r, 0.75, 0.0) + jnp.where(h_other == r, 0.25, 0.0)
        for half in range(2):
            at = pl.multiple_of(half * span + r * ROWS, ROWS)
            interp_ref[pl.ds(at, ROWS), :] = (col_weights[half] * weight).astype(BF16)
        return carry

    lax.fori_loop(0, z.coarse_rows, one_row, 0, unroll=z.coarse_rows <= 8)


def prepare_kernel(
    z, scale, cot_ref, other_ref, ws_ref, row_ref,
    d_hidden_ref, spread_ref, dskip_ref, interp_ref, bias_ref, tall_ref, flat_ref,
):
    blend = row_ref[:, z.cout :]
    interpolation(z, interp_ref)
    diagonal = ints((z.cout, z.cout), 0) == ints((z.cout, z.cout), 1)
    bias_ref[...] = jnp.sum(jnp.where(diagonal, row_ref[:, : z.cout], 0.0), axis=1, keepdims=True)
    lower = strips(z)[1]
    own, other = cot_ref[...].astype(F32), other_ref[...].astype(F32)
    count = z.cout * z.height
    tall_ref[:count, : z.width] = jnp.where(lower, own, other).reshape(count, z.width)
    tall_ref[count:, : z.width] = jnp.where(lower, other, own).reshape(count, z.width)
    back = jnp.concatenate([ws_ref[p, q] for p in range(3) for q in range(3)], axis=1)
    flat_ref[...] = jnp.zeros(flat_ref.shape, F32)
    for s in range(2):
        lanes = slice(s * z.lanes, (s + 1) * z.lanes)
        for h in range(z.height):
            piece = tall_ref[pl.ds(s * count + h, z.cout, stride=z.height), :]
            start = (h + 1) * z.pitch + 3
            flat_ref[:, start : start + z.width] = piece[:, : z.width]
        flat = flat_ref[...]
        d_second = (flat * (blend * scale)).astype(BF16).astype(F32)
        d_skip = pltpu.roll(flat * ((1.0 - blend) * scale), z.wide - (z.pitch + 1), 1)
        dskip_ref[:, lanes] = d_skip[:, : z.lanes].astype(BF16)
        for p in range(3):
            for q in range(3):
                start = (2 - q) * z.pitch + 2 - p
                moved = d_second if start == 0 else pltpu.roll(d_second, z.wide - start, 1)
                k = (p * 3 + q) * z.cout
                spread_ref[k : k + z.cout, lanes] = moved[:, : z.lanes].astype(BF16)
    d_hidden_ref[...] = jnp.dot(back, spread_ref[...], preferred_element_type=F32)


def holds_top(z):
    image, tile = lax.axis_index("img"), lax.axis_index("tile")
    bits = jnp.int32(0)
    for index, count in ((image, z.images), (tile, z.tiles)):
        k = 1
        while k < count:
            bits = bits ^ (lax.div(index, jnp.int32(k)) & 1)
            k *= 2
    return bits == 0


def main_kernel(
    z, got_ref, d_hidden_ref, spread_ref, dskip_ref, wf_ref, bias_ref, interp_ref,
    keep_ref, give_ref, up_ref, hidden_ref, taps_ref,
):
    tiles, lower = strips(z)
    n = ints((1, z.wide), 1) - 1
    w = n - (quotient(n + z.pitch, z.pitch) - 1) * z.pitch - 2
    m = ints((1, z.lanes), 1)
    mh = quotient(m, z.pitch)
    mw = m - mh * z.pitch - 2
    wanted = []
    for s in range(2):
        turned = got_ref[:, s * ROWS : (s + 1) * ROWS, :]
        turned = turned.reshape(z.coarse_rows * ROWS, 2 * z.cin).T
        windows = jnp.concatenate([turned[: z.cin], turned[z.cin :]], axis=1)
        up = jnp.dot(windows, interp_ref[...], preferred_element_type=F32)
        column = tiles[s] * z.width + w
        inside = jnp.where((column >= 0) & (column < z.width * z.tiles), 1.0, 0.0)
        up = (up * inside).astype(BF16).astype(F32)
        for p in range(3):
            for q in range(3):
                start = q * z.pitch + p
                moved = up if start == 0 else pltpu.roll(up, z.wide - start, 1)
                k = (p * 3 + q) * z.cin
                lanes = slice(s * z.lanes, (s + 1) * z.lanes)
                taps_ref[k : k + z.cin, lanes] = moved[:, : z.lanes].astype(BF16)
        column = tiles[s] * z.width + mw
        inside = (mw >= -1) & (mw <= z.width) & (mh < z.height)
        inside = inside & (column >= 0) & (column < z.width * z.tiles)
        wanted.append(jnp.where(inside, 1.0, 0.0))
    inside = jnp.concatenate(wanted, axis=1)
    taps = taps_ref[...]
    centre = taps_ref[4 * z.cin : 5 * z.cin, :]
    up_ref[...] = jnp.where(lower, centre[:, : z.lanes], centre[:, z.lanes :])
    kernel = jnp.concatenate([wf_ref[p, q] for p in range(3) for q in range(3)], axis=1)
    pre = jnp.dot(kernel, taps, preferred_element_type=F32) + bias_ref[...]
    sigma = 1.0 / (1.0 + jnp.exp(-pre))
    hidden = (pre * sigma * inside).astype(BF16)
    hidden_ref[...] = jnp.where(lower, hidden[:, : z.lanes], hidden[:, z.lanes :])
    slope = sigma * (1.0 + pre * (1.0 - sigma))
    d_pre = (d_hidden_ref[...] * slope * inside).astype(BF16)
    first = lax.dot_general(d_pre, taps, NT, preferred_element_type=F32)
    second = lax.dot_general(hidden, spread_ref[...], NT, preferred_element_type=F32)
    skip = lax.dot_general(dskip_ref[...], centre, NT, preferred_element_type=F32)
    ones = jnp.ones((z.cout, z.both), BF16)
    biases = lax.dot_general(ones, d_pre, NT, preferred_element_type=F32)
    full = keep_ref.shape[1]
    used = 10 * z.cin + 10 * z.cout
    pieces = [first, second, skip, biases]
    if full > used:
        pieces.append(jnp.zeros((z.cout, full - used), F32))
    grads = jnp.concatenate(pieces, axis=1)
    half = z.cout // 2
    top = holds_top(z)
    keep_ref[...] = jnp.where(top, grads[:half], grads[half:])
    give_ref[...] = jnp.where(top, grads[half:], grads[:half])


def blend_kernel(z, hidden_ref, up_ref, ws_ref, wk_ref, row_ref, out_ref, tall_ref):
    blend = row_ref[:, z.cout :]
    padded = jnp.concatenate(
        [hidden_ref[...].astype(F32), jnp.zeros((z.cout, z.wide - z.lanes), F32)], axis=1
    )
    padded = pltpu.roll(padded, z.pitch + 1, 1)
    taps = []
    for p in range(3):
        for q in range(3):
            start = q * z.pitch + p
            moved = padded if start == 0 else pltpu.roll(padded, z.wide - start, 1)
            taps.append(moved[:, : z.lanes].astype(BF16))
    taps = jnp.concatenate(taps, axis=0)
    kernel = ws_ref[...].reshape(9 * z.cout, z.cout).T
    second = jnp.dot(kernel, taps, preferred_element_type=F32)
    skip = jnp.dot(wk_ref[...], up_ref[...], preferred_element_type=F32)
    mixed = blend * second + (1.0 - blend) * skip
    for h in range(z.height):
        start = h * z.pitch + 2
        tall_ref[pl.ds(h, z.cout, stride=z.height), : z.width] = mixed[:, start : start + z.width]
    out_ref[...] = tall_ref[:, : z.width].reshape(out_ref.shape).astype(BF16)


def finish_kernel(z, mine_ref, other_ref, first_ref, bias_ref, second_ref, skip_ref):
    top = holds_top(z)
    mine, other = mine_ref[...], other_ref[...]
    total = jnp.concatenate(
        [jnp.where(top, mine, other), jnp.where(top, other, mine)], axis=0
    )
    at = 0
    for p in range(3):
        for q in range(3):
            first_ref[p, q] = total[:, at : at + z.cin]
            at += z.cin
    for p in range(3):
        for q in range(3):
            second_ref[p, q] = total[:, at : at + z.cout]
            at += z.cout
    skip_ref[...] = total[:, at : at + z.cin]
    at += z.cin
    bias_ref[...] = total[0:1, at : at + z.cout]


def call(body, outs, specs, scratch=(), flops=1000000):
    return pl.pallas_call(
        body,
        out_shape=outs,
        in_specs=specs,
        out_specs=jax.tree.map(lambda _: pl.BlockSpec(memory_space=pltpu.VMEM), outs),
        scratch_shapes=scratch,
        compiler_params=pltpu.CompilerParams(vmem_limit_bytes=48 * 1024 * 1024),
        cost_estimate=pl.CostEstimate(flops=flops, bytes_accessed=200000, transcendentals=0),
    )


def swap(values, images, tiles, across):
    a, b = across
    pairs = [
        (i * tiles + t, (i ^ a) * tiles + (t ^ b)) for i in range(images) for t in range(tiles)
    ]
    return lax.ppermute(values, ("img", "tile"), pairs)


def total_over_chips(mine, images, tiles):
    bits = []
    k = 2
    while k < images:
        bits.append((k, 0))
        k *= 2
    k = 1
    while k < tiles // 2:
        bits.append((0, k))
        k *= 2
    for at in range(0, len(bits), 2):
        group = bits[at : at + 2]
        sent = mine.astype(BF16)
        partners = [(a ^ 1, b) for a, b in group]
        if len(group) == 2:
            partners.append((group[0][0] ^ group[1][0], group[0][1] ^ group[1][1]))
        got = [swap(sent, images, tiles, across).astype(F32) for across in partners]
        mine = sent.astype(F32) + got[0]
        if len(got) == 3:
            mine = mine + (got[1] + got[2])
    return mine


def local(coarse, w_first, b_first, w_second, w_skip, fade_alpha, cotangent):
    tiles = lax.axis_size("tile")
    images = lax.axis_size("img")
    z = Sizes(coarse, cotangent, images, tiles)
    vmem = pl.BlockSpec(memory_space=pltpu.VMEM)
    bf, f32 = (lambda *s: jax.ShapeDtypeStruct(s, BF16)), (lambda *s: jax.ShapeDtypeStruct(s, F32))
    total_count = coarse.shape[0] * images * z.width * tiles * z.height
    scale = float(total_count) ** (-0.5)

    cot = jnp.transpose(cotangent[0], (0, 2, 1))
    wf = jnp.transpose(w_first, (0, 1, 3, 2))
    row = jnp.concatenate([b_first, fade_alpha]).reshape(1, z.cout + 1)
    other_cot = swap(cot, images, tiles, (0, z.pair))
    packed = call(
        functools.partial(pack_kernel, z), bf(tiles, 2 * ROWS, 2 * z.cin), [vmem]
    )(coarse.reshape(z.cin, z.coarse_cols))
    got = lax.all_to_all(packed, "tile", split_axis=0, concat_axis=0, tiled=True)

    d_hidden, spread, dskip, interp, bias = call(
        functools.partial(prepare_kernel, z, scale),
        (
            f32(z.cout, z.both),
            bf(9 * z.cout, z.both),
            bf(z.cout, z.both),
            bf(2 * z.coarse_rows * ROWS, z.wide),
            f32(z.cout, 1),
        ),
        [vmem] * 4,
        [pltpu.VMEM((2 * z.cout * z.height, 128), F32), pltpu.VMEM((z.cout, z.wide), F32)],
    )(cot, other_cot, w_second, row)

    columns = up128(10 * z.cin + 10 * z.cout)
    half = z.cout // 2
    keep, give, up, hidden = call(
        functools.partial(main_kernel, z),
        (f32(half, columns), f32(half, columns), bf(z.cin, z.lanes), bf(z.cout, z.lanes)),
        [vmem] * 7,
        [pltpu.VMEM((9 * z.cin, z.both), BF16)],
    )(got, d_hidden, spread, dskip, wf, bias, interp)

    blended = call(
        functools.partial(blend_kernel, z),
        bf(z.cout, z.height, z.width),
        [vmem] * 5,
        [pltpu.VMEM((z.cout * z.height, 128), F32)],
    )(hidden, up, w_second, jnp.transpose(w_skip), row)

    mine = keep + swap(give, images, tiles, (1, 0))
    mine = total_over_chips(mine, images, tiles)
    mine, blended = lax.optimization_barrier((mine, blended))
    other = swap(mine, images, tiles, (1, 0))
    first, bias, second, skip = call(
        functools.partial(finish_kernel, z),
        (f32(3, 3, z.cout, z.cin), f32(1, z.cout), f32(3, 3, z.cout, z.cout), f32(z.cout, z.cin)),
        [vmem] * 2,
    )(mine, other)
    return (
        jnp.transpose(blended, (0, 2, 1))[None],
        jnp.transpose(first, (0, 1, 3, 2)),
        bias.reshape(z.cout),
        second,
        jnp.transpose(skip),
    )


def solution(mesh):
    placed = (P("img", None, "tile", None), P(), P(), P(), P(), P(), P("img", None, "tile", None))
    return jax.shard_map(
        local,
        mesh=mesh,
        in_specs=placed,
        out_specs=(P("img", None, "tile", None), P(), P(), P(), P()),
        check_vma=False,
    )
```

```python
import functools

import jax
import jax.numpy as jnp
from jax import lax
from jax.experimental import pallas as pl
from jax.experimental.pallas import tpu as pltpu
from jax.sharding import PartitionSpec as P

F32 = jnp.float32
BF16 = jnp.bfloat16
ROWS = 16
NT = (((1,), (1,)), ((), ()))


def up128(n):
    return -(-n // 128) * 128


def ints(shape, dim):
    return lax.broadcasted_iota(jnp.int32, shape, dim)


def quotient(values, divisor):
    return ((values.astype(F32) + 0.5) * (1.0 / divisor)).astype(jnp.int32)


class Sizes:
    def __init__(self, coarse, cotangent, images, tiles):
        self.images = images
        self.tiles = tiles
        self.cin = coarse.shape[1]
        self.cout = cotangent.shape[1]
        self.coarse_rows = coarse.shape[2] * tiles
        self.coarse_cols = coarse.shape[3]
        self.own_coarse = self.coarse_cols // tiles
        self.width = cotangent.shape[2]
        self.height = cotangent.shape[3]
        self.pitch = self.width + 4
        self.window = self.own_coarse + 4
        self.half = self.window // 2
        self.lanes = up128(self.height * self.pitch)
        self.pair = tiles // 2
        self.wide = up128(self.lanes + 2 * self.pitch + 2)


def pack_kernel(z, coarse_ref, out_ref):
    row = coarse_ref[...]
    count = z.tiles * 2 * ROWS
    at = ints((count, z.coarse_cols), 0)
    col = ints((count, z.coarse_cols), 1)
    dest = lax.shift_right_logical(at, 5)
    strip = lax.bitwise_and(lax.shift_right_logical(at, 4), 1)
    tile = dest ^ (strip * z.pair)
    slot = lax.bitwise_and(at, ROWS - 1)
    parts = []
    for half in range(2):
        want = tile * z.own_coarse - 2 + half * z.half + slot
        want = jnp.clip(want, 0, z.coarse_cols - 1)
        pick = jnp.where((want == col) & (slot < z.half), 1.0, 0.0).astype(BF16)
        parts.append(lax.dot_general(pick, row, NT, preferred_element_type=F32))
    packed = jnp.concatenate(parts, axis=1).astype(BF16)
    out_ref[...] = packed.reshape(out_ref.shape)


def interpolation(z, interp_ref):
    n = ints((ROWS, z.wide), 1) - 1
    slot = ints((ROWS, z.wide), 0)
    h = quotient(n + z.pitch, z.pitch) - 2
    w = n - (h + 1) * z.pitch
    inside = (h >= 0) & (h < z.height)
    w_main = lax.shift_right_logical(w, 1) + 1
    w_other = w_main - 1 + 2 * lax.bitwise_and(w, 1)
    h_main = lax.shift_right_arithmetic(h, 1)
    h_other = jnp.clip(h_main - 1 + 2 * lax.bitwise_and(h, 1), 0, z.coarse_rows - 1)
    col_weights = []
    for half in range(2):
        at = slot + half * z.half
        weight = jnp.where(at == w_main, 0.75, 0.0) + jnp.where(at == w_other, 0.25, 0.0)
        col_weights.append(jnp.where(inside & (slot < z.half), weight, 0.0))
    span = z.coarse_rows * ROWS

    def one_row(r, carry):
        weight = jnp.where(h_main == r, 0.75, 0.0) + jnp.where(h_other == r, 0.25, 0.0)
        for half in range(2):
            at = pl.multiple_of(half * span + r * ROWS, ROWS)
            interp_ref[pl.ds(at, ROWS), :] = (col_weights[half] * weight).astype(BF16)
        return carry

    lax.fori_loop(0, z.coarse_rows, one_row, 0, unroll=z.coarse_rows <= 8)


def flatten_kernel(z, cot_ref, flat_ref, tall_ref, wide_ref):
    tall_ref[:, : z.width] = cot_ref[...].astype(F32).reshape(z.cout * z.height, z.width)
    wide_ref[...] = jnp.zeros(wide_ref.shape, F32)
    for h in range(z.height):
        piece = tall_ref[pl.ds(h, z.cout, stride=z.height), :]
        start = h * z.pitch + 2
        wide_ref[:, start : start + z.width] = piece[:, : z.width]
    flat_ref[...] = wide_ref[...].astype(BF16)


def backward(z, scale, flat_ref, ws_ref, row_ref, spread_ref):
    blend = row_ref[:, z.cout :]
    flat = flat_ref[...].astype(F32)
    d_skip = (flat * ((1.0 - blend) * scale)).astype(BF16)
    d_second = (flat * (blend * scale)).astype(BF16).astype(F32)
    d_second = jnp.concatenate([d_second, jnp.zeros((z.cout, z.wide - z.lanes), F32)], axis=1)
    back = []
    for p in range(3):
        for q in range(3):
            shift = (q - 1) * z.pitch + p - 1
            moved = d_second if shift == 0 else pltpu.roll(d_second, shift % z.wide, 1)
            k = (p * 3 + q) * z.cout
            spread_ref[k : k + z.cout, :] = moved[:, : z.lanes].astype(BF16)
            back.append(ws_ref[p, q])
    d_hidden = jnp.dot(
        jnp.concatenate(back, axis=1), spread_ref[...], preferred_element_type=F32
    )
    return d_skip, d_hidden


def prepare_kernel(
    z, scale, flat_ref, ws_ref, row_ref, d_hidden_ref, spread_ref, dskip_ref, interp_ref, bias_ref
):
    interpolation(z, interp_ref)
    diagonal = ints((z.cout, z.cout), 0) == ints((z.cout, z.cout), 1)
    bias_ref[...] = jnp.sum(jnp.where(diagonal, row_ref[:, : z.cout], 0.0), axis=1, keepdims=True)
    d_skip, d_hidden = backward(z, scale, flat_ref, ws_ref, row_ref, spread_ref)
    dskip_ref[...] = d_skip
    d_hidden_ref[...] = d_hidden


def holds_top(z):
    image, tile = lax.axis_index("img"), lax.axis_index("tile")
    bits = jnp.int32(0)
    for index, count in ((image, z.images), (tile, z.tiles)):
        k = 1
        while k < count:
            bits = bits ^ (lax.div(index, jnp.int32(k)) & 1)
            k *= 2
    return bits == 0


def gradients(z, d_hidden, d_skip, spread, slope, hidden, taps, centre):
    d_pre = (d_hidden * slope).astype(BF16)
    first = lax.dot_general(d_pre, taps, NT, preferred_element_type=F32)
    second = lax.dot_general(hidden, spread, NT, preferred_element_type=F32)
    skip = lax.dot_general(d_skip, centre, NT, preferred_element_type=F32)
    ones = jnp.ones((z.cout, z.lanes), BF16)
    biases = lax.dot_general(ones, d_pre, NT, preferred_element_type=F32)
    return jnp.concatenate([first, second, skip, biases], axis=1)


def forward_kernel(
    z, got_ref, d_hidden_ref, spread_ref, dskip_ref, wf_ref, bias_ref, interp_ref,
    sums_ref, up_ref, hidden_ref, other_taps_ref, other_hidden_ref, other_slope_ref, taps_ref,
):
    position = lax.axis_index("tile")
    n = ints((1, z.wide), 1) - 1
    w = n - (quotient(n + z.pitch, z.pitch) - 1) * z.pitch - 2
    m = ints((1, z.lanes), 1)
    mh = quotient(m, z.pitch)
    mw = m - mh * z.pitch - 2
    kernel = jnp.concatenate([wf_ref[p, q] for p in range(3) for q in range(3)], axis=1)
    for s, here_ref in enumerate((taps_ref, other_taps_ref)):
        tile = position ^ (s * z.pair)
        turned = got_ref[:, s * ROWS : (s + 1) * ROWS, :]
        turned = turned.reshape(z.coarse_rows * ROWS, 2 * z.cin).T
        windows = jnp.concatenate([turned[: z.cin], turned[z.cin :]], axis=1)
        up = jnp.dot(windows, interp_ref[...], preferred_element_type=F32)
        column = tile * z.width + w
        inside = jnp.where((column >= 0) & (column < z.width * z.tiles), 1.0, 0.0)
        up = (up * inside).astype(BF16).astype(F32)
        for p in range(3):
            for q in range(3):
                start = q * z.pitch + p
                moved = up if start == 0 else pltpu.roll(up, z.wide - start, 1)
                k = (p * 3 + q) * z.cin
                here_ref[k : k + z.cin, :] = moved[:, : z.lanes].astype(BF16)
        column = tile * z.width + mw
        inside = (mw >= -1) & (mw <= z.width) & (mh < z.height)
        inside = inside & (column >= 0) & (column < z.width * z.tiles)
        inside = jnp.where(inside, 1.0, 0.0)
        taps = here_ref[...]
        pre = jnp.dot(kernel, taps, preferred_element_type=F32) + bias_ref[...]
        sigma = 1.0 / (1.0 + jnp.exp(-pre))
        hidden = (pre * sigma * inside).astype(BF16)
        slope = sigma * (1.0 + pre * (1.0 - sigma)) * inside
        if s == 0:
            centre = here_ref[4 * z.cin : 5 * z.cin, :]
            up_ref[...] = centre
            hidden_ref[...] = hidden
            sums_ref[...] = gradients(
                z, d_hidden_ref[...], dskip_ref[...], spread_ref[...], slope, hidden, taps, centre
            )
        else:
            other_hidden_ref[...] = hidden
            other_slope_ref[...] = slope


def other_kernel(
    z, scale, sums_ref, taps_ref, hidden_ref, slope_ref, flat_ref, ws_ref, row_ref,
    keep_ref, give_ref, spread_ref,
):
    d_skip, d_hidden = backward(z, scale, flat_ref, ws_ref, row_ref, spread_ref)
    centre = taps_ref[4 * z.cin : 5 * z.cin, :]
    grads = sums_ref[...] + gradients(
        z, d_hidden, d_skip, spread_ref[...], slope_ref[...], hidden_ref[...], taps_ref[...], centre
    )
    full, used = keep_ref.shape[1], grads.shape[1]
    if full > used:
        grads = jnp.concatenate([grads, jnp.zeros((z.cout, full - used), F32)], axis=1)
    half = z.cout // 2
    top = holds_top(z)
    keep_ref[...] = jnp.where(top, grads[:half], grads[half:])
    give_ref[...] = jnp.where(top, grads[half:], grads[:half])


def blend_kernel(z, hidden_ref, up_ref, ws_ref, wk_ref, row_ref, out_ref, tall_ref):
    blend = row_ref[:, z.cout :]
    padded = jnp.concatenate(
        [hidden_ref[...].astype(F32), jnp.zeros((z.cout, z.wide - z.lanes), F32)], axis=1
    )
    padded = pltpu.roll(padded, z.pitch + 1, 1)
    taps = []
    for p in range(3):
        for q in range(3):
            start = q * z.pitch + p
            moved = padded if start == 0 else pltpu.roll(padded, z.wide - start, 1)
            taps.append(moved[:, : z.lanes].astype(BF16))
    taps = jnp.concatenate(taps, axis=0)
    kernel = ws_ref[...].reshape(9 * z.cout, z.cout).T
    second = jnp.dot(kernel, taps, preferred_element_type=F32)
    skip = jnp.dot(wk_ref[...], up_ref[...], preferred_element_type=F32)
    mixed = blend * second + (1.0 - blend) * skip
    for h in range(z.height):
        start = h * z.pitch + 2
        tall_ref[pl.ds(h, z.cout, stride=z.height), : z.width] = mixed[:, start : start + z.width]
    out_ref[...] = tall_ref[:, : z.width].reshape(out_ref.shape).astype(BF16)


def finish_kernel(z, mine_ref, other_ref, first_ref, bias_ref, second_ref, skip_ref):
    top = holds_top(z)
    mine, other = mine_ref[...], other_ref[...]
    total = jnp.concatenate(
        [jnp.where(top, mine, other), jnp.where(top, other, mine)], axis=0
    )
    at = 0
    for p in range(3):
        for q in range(3):
            first_ref[p, q] = total[:, at : at + z.cin]
            at += z.cin
    for p in range(3):
        for q in range(3):
            second_ref[p, q] = total[:, at : at + z.cout]
            at += z.cout
    skip_ref[...] = total[:, at : at + z.cin]
    at += z.cin
    bias_ref[...] = total[0:1, at : at + z.cout]


def call(body, outs, specs, scratch=(), flops=1000000):
    return pl.pallas_call(
        body,
        out_shape=outs,
        in_specs=specs,
        out_specs=jax.tree.map(lambda _: pl.BlockSpec(memory_space=pltpu.VMEM), outs),
        scratch_shapes=scratch,
        compiler_params=pltpu.CompilerParams(vmem_limit_bytes=48 * 1024 * 1024),
        cost_estimate=pl.CostEstimate(flops=flops, bytes_accessed=200000, transcendentals=0),
    )


def swap(values, images, tiles, across):
    a, b = across
    pairs = [
        (i * tiles + t, (i ^ a) * tiles + (t ^ b)) for i in range(images) for t in range(tiles)
    ]
    return lax.ppermute(values, ("img", "tile"), pairs)


def total_over_chips(mine, images, tiles):
    bits = []
    k = 2
    while k < images:
        bits.append((k, 0))
        k *= 2
    k = 1
    while k < tiles // 2:
        bits.append((0, k))
        k *= 2
    for at in range(0, len(bits), 2):
        group = bits[at : at + 2]
        sent = mine.astype(BF16)
        partners = [(a ^ 1, b) for a, b in group]
        if len(group) == 2:
            partners.append((group[0][0] ^ group[1][0], group[0][1] ^ group[1][1]))
        got = [swap(sent, images, tiles, across).astype(F32) for across in partners]
        mine = sent.astype(F32) + got[0]
        if len(got) == 3:
            mine = mine + (got[1] + got[2])
    return mine


def local(coarse, w_first, b_first, w_second, w_skip, fade_alpha, cotangent):
    tiles = lax.axis_size("tile")
    images = lax.axis_size("img")
    z = Sizes(coarse, cotangent, images, tiles)
    vmem = pl.BlockSpec(memory_space=pltpu.VMEM)
    bf, f32 = (lambda *s: jax.ShapeDtypeStruct(s, BF16)), (lambda *s: jax.ShapeDtypeStruct(s, F32))
    total_count = coarse.shape[0] * images * z.width * tiles * z.height
    scale = float(total_count) ** (-0.5)

    packed = call(
        functools.partial(pack_kernel, z), bf(tiles, 2 * ROWS, 2 * z.cin), [vmem]
    )(coarse.reshape(z.cin, z.coarse_cols))
    got = lax.all_to_all(packed, "tile", split_axis=0, concat_axis=0, tiled=True)

    flat = call(
        functools.partial(flatten_kernel, z),
        bf(z.cout, z.lanes),
        [vmem],
        [pltpu.VMEM((z.cout * z.height, 128), F32), pltpu.VMEM((z.cout, z.lanes), F32)],
    )(jnp.transpose(cotangent[0], (0, 2, 1)))
    other_flat = swap(flat, images, tiles, (0, z.pair))
    row = jnp.concatenate([b_first, fade_alpha]).reshape(1, z.cout + 1)
    d_hidden, spread, dskip, interp, bias = call(
        functools.partial(prepare_kernel, z, scale),
        (
            f32(z.cout, z.lanes),
            bf(9 * z.cout, z.lanes),
            bf(z.cout, z.lanes),
            bf(2 * z.coarse_rows * ROWS, z.wide),
            f32(z.cout, 1),
        ),
        [vmem] * 3,
    )(flat, w_second, row)

    used = 10 * z.cin + 10 * z.cout
    sums, up, hidden, *other = call(
        functools.partial(forward_kernel, z),
        (
            f32(z.cout, used),
            bf(z.cin, z.lanes),
            bf(z.cout, z.lanes),
            bf(9 * z.cin, z.lanes),
            bf(z.cout, z.lanes),
            f32(z.cout, z.lanes),
        ),
        [vmem] * 7,
        [pltpu.VMEM((9 * z.cin, z.lanes), BF16)],
    )(got, d_hidden, spread, dskip, jnp.transpose(w_first, (0, 1, 3, 2)), bias, interp)

    half = f32(z.cout // 2, up128(used))
    keep, give = call(
        functools.partial(other_kernel, z, scale),
        (half, half),
        [vmem] * 7,
        [pltpu.VMEM((9 * z.cout, z.lanes), BF16)],
    )(sums, *other, other_flat, w_second, row)

    blended = call(
        functools.partial(blend_kernel, z),
        bf(z.cout, z.height, z.width),
        [vmem] * 5,
        [pltpu.VMEM((z.cout * z.height, 128), F32)],
    )(hidden, up, w_second, jnp.transpose(w_skip), row)

    mine = keep + swap(give, images, tiles, (1, 0))
    mine = total_over_chips(mine, images, tiles)
    mine, blended = lax.optimization_barrier((mine, blended))
    other = swap(mine, images, tiles, (1, 0))
    first, bias, second, skip = call(
        functools.partial(finish_kernel, z),
        (f32(3, 3, z.cout, z.cin), f32(1, z.cout), f32(3, 3, z.cout, z.cout), f32(z.cout, z.cin)),
        [vmem] * 2,
    )(mine, other)
    return (
        jnp.transpose(blended, (0, 2, 1))[None],
        jnp.transpose(first, (0, 1, 3, 2)),
        bias.reshape(z.cout),
        second,
        jnp.transpose(skip),
    )


def solution(mesh):
    placed = (P("img", None, "tile", None), P(), P(), P(), P(), P(), P("img", None, "tile", None))
    return jax.shard_map(
        local,
        mesh=mesh,
        in_specs=placed,
        out_specs=(P("img", None, "tile", None), P(), P(), P(), P()),
        check_vma=False,
    )
```

```python
import functools

import jax
import jax.numpy as jnp
from jax import lax
from jax.experimental import pallas as pl
from jax.experimental.pallas import tpu as pltpu
from jax.sharding import PartitionSpec as P

F32 = jnp.float32
BF16 = jnp.bfloat16
ROWS = 16
NT = (((1,), (1,)), ((), ()))


def up128(n):
    return -(-n // 128) * 128


def ints(shape, dim):
    return lax.broadcasted_iota(jnp.int32, shape, dim)


def quotient(values, divisor):
    return ((values.astype(F32) + 0.5) * (1.0 / divisor)).astype(jnp.int32)


class Sizes:
    def __init__(self, coarse, cotangent, images, tiles):
        self.images = images
        self.tiles = tiles
        self.cin = coarse.shape[1]
        self.cout = cotangent.shape[1]
        self.coarse_rows = coarse.shape[2] * tiles
        self.coarse_cols = coarse.shape[3]
        self.own_coarse = self.coarse_cols // tiles
        self.width = cotangent.shape[2]
        self.height = cotangent.shape[3]
        self.pitch = self.width + 4
        self.window = self.own_coarse + 4
        self.half = self.window // 2
        self.lanes = up128(self.height * self.pitch)
        self.pair = tiles // 2
        self.wide = up128(self.lanes + 2 * self.pitch + 2)


def pack_kernel(z, coarse_ref, out_ref):
    row = coarse_ref[...]
    count = z.tiles * 2 * ROWS
    at = ints((count, z.coarse_cols), 0)
    col = ints((count, z.coarse_cols), 1)
    dest = lax.shift_right_logical(at, 5)
    strip = lax.bitwise_and(lax.shift_right_logical(at, 4), 1)
    tile = dest ^ (strip * z.pair)
    slot = lax.bitwise_and(at, ROWS - 1)
    parts = []
    for half in range(2):
        want = tile * z.own_coarse - 2 + half * z.half + slot
        want = jnp.clip(want, 0, z.coarse_cols - 1)
        pick = jnp.where((want == col) & (slot < z.half), 1.0, 0.0).astype(BF16)
        parts.append(lax.dot_general(pick, row, NT, preferred_element_type=F32))
    packed = jnp.concatenate(parts, axis=1).astype(BF16)
    out_ref[...] = packed.reshape(out_ref.shape)


def interpolation(z, interp_ref):
    n = ints((ROWS, z.wide), 1) - 1
    slot = ints((ROWS, z.wide), 0)
    h = quotient(n + z.pitch, z.pitch) - 2
    w = n - (h + 1) * z.pitch
    inside = (h >= 0) & (h < z.height)
    w_main = lax.shift_right_logical(w, 1) + 1
    w_other = w_main - 1 + 2 * lax.bitwise_and(w, 1)
    h_main = lax.shift_right_arithmetic(h, 1)
    h_other = jnp.clip(h_main - 1 + 2 * lax.bitwise_and(h, 1), 0, z.coarse_rows - 1)
    col_weights = []
    for half in range(2):
        at = slot + half * z.half
        weight = jnp.where(at == w_main, 0.75, 0.0) + jnp.where(at == w_other, 0.25, 0.0)
        col_weights.append(jnp.where(inside & (slot < z.half), weight, 0.0))
    span = z.coarse_rows * ROWS

    def one_row(r, carry):
        weight = jnp.where(h_main == r, 0.75, 0.0) + jnp.where(h_other == r, 0.25, 0.0)
        for half in range(2):
            at = pl.multiple_of(half * span + r * ROWS, ROWS)
            interp_ref[pl.ds(at, ROWS), :] = (col_weights[half] * weight).astype(BF16)
        return carry

    lax.fori_loop(0, z.coarse_rows, one_row, 0, unroll=z.coarse_rows <= 8)


def flatten_kernel(z, cot_ref, flat_ref, tall_ref, wide_ref):
    tall_ref[:, : z.width] = cot_ref[...].astype(F32).reshape(z.cout * z.height, z.width)
    wide_ref[...] = jnp.zeros(wide_ref.shape, F32)
    for h in range(z.height):
        piece = tall_ref[pl.ds(h, z.cout, stride=z.height), :]
        start = h * z.pitch + 2
        wide_ref[:, start : start + z.width] = piece[:, : z.width]
    flat_ref[...] = wide_ref[...].astype(BF16)


def backward(z, scale, flat_ref, ws_ref, row_ref, spread_ref):
    blend = row_ref[:, z.cout :]
    flat = flat_ref[...].astype(F32)
    d_skip = (flat * ((1.0 - blend) * scale)).astype(BF16)
    d_second = (flat * (blend * scale)).astype(BF16).astype(F32)
    d_second = jnp.concatenate([d_second, jnp.zeros((z.cout, z.wide - z.lanes), F32)], axis=1)
    back = []
    for p in range(3):
        for q in range(3):
            shift = (q - 1) * z.pitch + p - 1
            moved = d_second if shift == 0 else pltpu.roll(d_second, shift % z.wide, 1)
            k = (p * 3 + q) * z.cout
            spread_ref[k : k + z.cout, :] = moved[:, : z.lanes].astype(BF16)
            back.append(ws_ref[p, q])
    d_hidden = jnp.dot(
        jnp.concatenate(back, axis=1), spread_ref[...], preferred_element_type=F32
    )
    return d_skip, d_hidden


def prepare_kernel(
    z, scale, flat_ref, ws_ref, row_ref, d_hidden_ref, spread_ref, dskip_ref, interp_ref, bias_ref
):
    interpolation(z, interp_ref)
    diagonal = ints((z.cout, z.cout), 0) == ints((z.cout, z.cout), 1)
    bias_ref[...] = jnp.sum(jnp.where(diagonal, row_ref[:, : z.cout], 0.0), axis=1, keepdims=True)
    d_skip, d_hidden = backward(z, scale, flat_ref, ws_ref, row_ref, spread_ref)
    dskip_ref[...] = d_skip
    d_hidden_ref[...] = d_hidden


def holds_top(z):
    image, tile = lax.axis_index("img"), lax.axis_index("tile")
    bits = jnp.int32(0)
    for index, count in ((image, z.images), (tile, z.tiles)):
        k = 1
        while k < count:
            bits = bits ^ (lax.div(index, jnp.int32(k)) & 1)
            k *= 2
    return bits == 0


def gradients(z, d_hidden, d_skip, spread, slope, hidden, taps, centre):
    d_pre = (d_hidden * slope).astype(BF16)
    first = lax.dot_general(d_pre, taps, NT, preferred_element_type=F32)
    second = lax.dot_general(hidden, spread, NT, preferred_element_type=F32)
    skip = lax.dot_general(d_skip, centre, NT, preferred_element_type=F32)
    ones = jnp.ones((z.cout, z.lanes), BF16)
    biases = lax.dot_general(ones, d_pre, NT, preferred_element_type=F32)
    return jnp.concatenate([first, second, skip, biases], axis=1)


def forward_kernel(
    z, got_ref, d_hidden_ref, spread_ref, dskip_ref, wf_ref, bias_ref, interp_ref,
    sums_ref, up_ref, hidden_ref, other_taps_ref, other_hidden_ref, other_slope_ref, taps_ref,
):
    position = lax.axis_index("tile")
    n = ints((1, z.wide), 1) - 1
    w = n - (quotient(n + z.pitch, z.pitch) - 1) * z.pitch - 2
    m = ints((1, z.lanes), 1)
    mh = quotient(m, z.pitch)
    mw = m - mh * z.pitch - 2
    kernel = jnp.concatenate([wf_ref[p, q] for p in range(3) for q in range(3)], axis=1)
    for s, here_ref in enumerate((taps_ref, other_taps_ref)):
        tile = position ^ (s * z.pair)
        turned = got_ref[:, s * ROWS : (s + 1) * ROWS, :]
        turned = turned.reshape(z.coarse_rows * ROWS, 2 * z.cin).T
        windows = jnp.concatenate([turned[: z.cin], turned[z.cin :]], axis=1)
        up = jnp.dot(windows, interp_ref[...], preferred_element_type=F32)
        column = tile * z.width + w
        inside = jnp.where((column >= 0) & (column < z.width * z.tiles), 1.0, 0.0)
        up = (up * inside).astype(BF16).astype(F32)
        for p in range(3):
            for q in range(3):
                start = q * z.pitch + p
                moved = up if start == 0 else pltpu.roll(up, z.wide - start, 1)
                k = (p * 3 + q) * z.cin
                here_ref[k : k + z.cin, :] = moved[:, : z.lanes].astype(BF16)
        column = tile * z.width + mw
        inside = (mw >= -1) & (mw <= z.width) & (mh < z.height)
        inside = inside & (column >= 0) & (column < z.width * z.tiles)
        inside = jnp.where(inside, 1.0, 0.0)
        taps = here_ref[...]
        pre = jnp.dot(kernel, taps, preferred_element_type=F32) + bias_ref[...]
        sigma = 1.0 / (1.0 + jnp.exp(-pre))
        hidden = (pre * sigma * inside).astype(BF16)
        slope = sigma * (1.0 + pre * (1.0 - sigma)) * inside
        if s == 0:
            centre = here_ref[4 * z.cin : 5 * z.cin, :]
            up_ref[...] = centre
            hidden_ref[...] = hidden
            sums_ref[...] = gradients(
                z, d_hidden_ref[...], dskip_ref[...], spread_ref[...], slope, hidden, taps, centre
            )
        else:
            other_hidden_ref[...] = hidden
            other_slope_ref[...] = slope


def other_kernel(
    z, scale, sums_ref, taps_ref, hidden_ref, slope_ref, flat_ref, ws_ref, row_ref,
    keep_ref, give_ref, spread_ref,
):
    d_skip, d_hidden = backward(z, scale, flat_ref, ws_ref, row_ref, spread_ref)
    centre = taps_ref[4 * z.cin : 5 * z.cin, :]
    grads = sums_ref[...] + gradients(
        z, d_hidden, d_skip, spread_ref[...], slope_ref[...], hidden_ref[...], taps_ref[...], centre
    )
    full, used = keep_ref.shape[1], grads.shape[1]
    if full > used:
        grads = jnp.concatenate([grads, jnp.zeros((z.cout, full - used), F32)], axis=1)
    half = z.cout // 2
    top = holds_top(z)
    keep_ref[...] = jnp.where(top, grads[:half], grads[half:])
    give_ref[...] = jnp.where(top, grads[half:], grads[:half])


def blend_kernel(z, hidden_ref, up_ref, ws_ref, wk_ref, row_ref, out_ref, tall_ref):
    blend = row_ref[:, z.cout :]
    padded = jnp.concatenate(
        [hidden_ref[...].astype(F32), jnp.zeros((z.cout, z.wide - z.lanes), F32)], axis=1
    )
    padded = pltpu.roll(padded, z.pitch + 1, 1)
    taps = []
    for p in range(3):
        for q in range(3):
            start = q * z.pitch + p
            moved = padded if start == 0 else pltpu.roll(padded, z.wide - start, 1)
            taps.append(moved[:, : z.lanes].astype(BF16))
    taps = jnp.concatenate(taps, axis=0)
    kernel = ws_ref[...].reshape(9 * z.cout, z.cout).T
    second = jnp.dot(kernel, taps, preferred_element_type=F32)
    skip = jnp.dot(wk_ref[...], up_ref[...], preferred_element_type=F32)
    mixed = blend * second + (1.0 - blend) * skip
    for h in range(z.height):
        start = h * z.pitch + 2
        tall_ref[pl.ds(h, z.cout, stride=z.height), : z.width] = mixed[:, start : start + z.width]
    out_ref[...] = tall_ref[:, : z.width].reshape(out_ref.shape).astype(BF16)


def finish_kernel(z, mine_ref, other_ref, first_ref, bias_ref, second_ref, skip_ref):
    top = holds_top(z)
    mine, other = mine_ref[...], other_ref[...]
    total = jnp.concatenate(
        [jnp.where(top, mine, other), jnp.where(top, other, mine)], axis=0
    )
    at = 0
    for p in range(3):
        for q in range(3):
            first_ref[p, q] = total[:, at : at + z.cin]
            at += z.cin
    for p in range(3):
        for q in range(3):
            second_ref[p, q] = total[:, at : at + z.cout]
            at += z.cout
    skip_ref[...] = total[:, at : at + z.cin]
    at += z.cin
    bias_ref[...] = total[0:1, at : at + z.cout]


def call(body, outs, specs, scratch=(), flops=1000000):
    return pl.pallas_call(
        body,
        out_shape=outs,
        in_specs=specs,
        out_specs=jax.tree.map(lambda _: pl.BlockSpec(memory_space=pltpu.VMEM), outs),
        scratch_shapes=scratch,
        compiler_params=pltpu.CompilerParams(vmem_limit_bytes=48 * 1024 * 1024),
        cost_estimate=pl.CostEstimate(flops=flops, bytes_accessed=200000, transcendentals=0),
    )


def swap(values, images, tiles, across):
    a, b = across
    pairs = [
        (i * tiles + t, (i ^ a) * tiles + (t ^ b)) for i in range(images) for t in range(tiles)
    ]
    return lax.ppermute(values, ("img", "tile"), pairs)


def total_over_chips(mine, images, tiles):
    bits = []
    k = 2
    while k < images:
        bits.append((k, 0))
        k *= 2
    k = 1
    while k < tiles // 2:
        bits.append((0, k))
        k *= 2
    odd = len(bits) % 2
    groups = [bits[:odd]] if odd else []
    groups += [(bits[at + 1], bits[at]) for at in range(odd, len(bits), 2)]
    for group in groups:
        sent = mine.astype(BF16)
        partners = [(a ^ 1, b) for a, b in group]
        if len(group) == 2:
            partners.append((group[0][0] ^ group[1][0], group[0][1] ^ group[1][1]))
        got = [swap(sent, images, tiles, across).astype(F32) for across in partners]
        mine = sent.astype(F32) + got[0]
        if len(got) == 3:
            mine = mine + (got[1] + got[2])
    return mine


def local(coarse, w_first, b_first, w_second, w_skip, fade_alpha, cotangent):
    tiles = lax.axis_size("tile")
    images = lax.axis_size("img")
    z = Sizes(coarse, cotangent, images, tiles)
    vmem = pl.BlockSpec(memory_space=pltpu.VMEM)
    bf, f32 = (lambda *s: jax.ShapeDtypeStruct(s, BF16)), (lambda *s: jax.ShapeDtypeStruct(s, F32))
    total_count = coarse.shape[0] * images * z.width * tiles * z.height
    scale = float(total_count) ** (-0.5)

    packed = call(
        functools.partial(pack_kernel, z), bf(tiles, 2 * ROWS, 2 * z.cin), [vmem]
    )(coarse.reshape(z.cin, z.coarse_cols))
    got = lax.all_to_all(packed, "tile", split_axis=0, concat_axis=0, tiled=True)

    flat = call(
        functools.partial(flatten_kernel, z),
        bf(z.cout, z.lanes),
        [vmem],
        [pltpu.VMEM((z.cout * z.height, 128), F32), pltpu.VMEM((z.cout, z.lanes), F32)],
    )(jnp.transpose(cotangent[0], (0, 2, 1)))
    other_flat = swap(flat, images, tiles, (0, z.pair))
    row = jnp.concatenate([b_first, fade_alpha]).reshape(1, z.cout + 1)
    d_hidden, spread, dskip, interp, bias = call(
        functools.partial(prepare_kernel, z, scale),
        (
            f32(z.cout, z.lanes),
            bf(9 * z.cout, z.lanes),
            bf(z.cout, z.lanes),
            bf(2 * z.coarse_rows * ROWS, z.wide),
            f32(z.cout, 1),
        ),
        [vmem] * 3,
    )(flat, w_second, row)

    used = 10 * z.cin + 10 * z.cout
    sums, up, hidden, *other = call(
        functools.partial(forward_kernel, z),
        (
            f32(z.cout, used),
            bf(z.cin, z.lanes),
            bf(z.cout, z.lanes),
            bf(9 * z.cin, z.lanes),
            bf(z.cout, z.lanes),
            f32(z.cout, z.lanes),
        ),
        [vmem] * 7,
        [pltpu.VMEM((9 * z.cin, z.lanes), BF16)],
    )(got, d_hidden, spread, dskip, jnp.transpose(w_first, (0, 1, 3, 2)), bias, interp)

    half = f32(z.cout // 2, up128(used))
    keep, give = call(
        functools.partial(other_kernel, z, scale),
        (half, half),
        [vmem] * 7,
        [pltpu.VMEM((9 * z.cout, z.lanes), BF16)],
    )(sums, *other, other_flat, w_second, row)

    blended = call(
        functools.partial(blend_kernel, z),
        bf(z.cout, z.height, z.width),
        [vmem] * 5,
        [pltpu.VMEM((z.cout * z.height, 128), F32)],
    )(hidden, up, w_second, jnp.transpose(w_skip), row)

    mine = keep + swap(give, images, tiles, (1, 0))
    mine = total_over_chips(mine, images, tiles)
    mine, blended = lax.optimization_barrier((mine, blended))
    other = swap(mine, images, tiles, (1, 0))
    first, bias, second, skip = call(
        functools.partial(finish_kernel, z),
        (f32(3, 3, z.cout, z.cin), f32(1, z.cout), f32(3, 3, z.cout, z.cout), f32(z.cout, z.cin)),
        [vmem] * 2,
    )(mine, other)
    return (
        jnp.transpose(blended, (0, 2, 1))[None],
        jnp.transpose(first, (0, 1, 3, 2)),
        bias.reshape(z.cout),
        second,
        jnp.transpose(skip),
    )


def solution(mesh):
    placed = (P("img", None, "tile", None), P(), P(), P(), P(), P(), P("img", None, "tile", None))
    return jax.shard_map(
        local,
        mesh=mesh,
        in_specs=placed,
        out_specs=(P("img", None, "tile", None), P(), P(), P(), P()),
        check_vma=False,
    )
```

```python
import functools

import jax
import jax.numpy as jnp
from jax import lax
from jax.experimental import pallas as pl
from jax.experimental.pallas import tpu as pltpu
from jax.sharding import PartitionSpec as P

F32 = jnp.float32
BF16 = jnp.bfloat16
ROWS = 16
NT = (((1,), (1,)), ((), ()))


def up128(n):
    return -(-n // 128) * 128


def ints(shape, dim):
    return lax.broadcasted_iota(jnp.int32, shape, dim)


def quotient(values, divisor):
    return ((values.astype(F32) + 0.5) * (1.0 / divisor)).astype(jnp.int32)


class Sizes:
    def __init__(self, coarse, cotangent, images, tiles):
        self.images = images
        self.tiles = tiles
        self.cin = coarse.shape[1]
        self.cout = cotangent.shape[1]
        self.coarse_rows = coarse.shape[2] * tiles
        self.coarse_cols = coarse.shape[3]
        self.own_coarse = self.coarse_cols // tiles
        self.width = cotangent.shape[2]
        self.height = cotangent.shape[3]
        self.pitch = self.width + 4
        self.window = self.own_coarse + 4
        self.half = self.window // 2
        self.lanes = up128(self.height * self.pitch)
        self.pair = tiles // 2
        self.wide = up128(self.lanes + 2 * self.pitch + 2)


def pack_kernel(z, coarse_ref, out_ref):
    row = coarse_ref[...]
    count = z.tiles * 2 * ROWS
    at = ints((count, z.coarse_cols), 0)
    col = ints((count, z.coarse_cols), 1)
    dest = lax.shift_right_logical(at, 5)
    strip = lax.bitwise_and(lax.shift_right_logical(at, 4), 1)
    tile = dest ^ (strip * z.pair)
    slot = lax.bitwise_and(at, ROWS - 1)
    parts = []
    for half in range(2):
        want = tile * z.own_coarse - 2 + half * z.half + slot
        want = jnp.clip(want, 0, z.coarse_cols - 1)
        pick = jnp.where((want == col) & (slot < z.half), 1.0, 0.0).astype(BF16)
        parts.append(lax.dot_general(pick, row, NT, preferred_element_type=F32))
    packed = jnp.concatenate(parts, axis=1).astype(BF16)
    out_ref[...] = packed.reshape(out_ref.shape)


def interpolation(z, interp_ref):
    n = ints((ROWS, z.wide), 1) - 1
    slot = ints((ROWS, z.wide), 0)
    h = quotient(n + z.pitch, z.pitch) - 2
    w = n - (h + 1) * z.pitch
    inside = (h >= 0) & (h < z.height)
    w_main = lax.shift_right_logical(w, 1) + 1
    w_other = w_main - 1 + 2 * lax.bitwise_and(w, 1)
    h_main = lax.shift_right_arithmetic(h, 1)
    h_other = jnp.clip(h_main - 1 + 2 * lax.bitwise_and(h, 1), 0, z.coarse_rows - 1)
    col_weights = []
    for half in range(2):
        at = slot + half * z.half
        weight = jnp.where(at == w_main, 0.75, 0.0) + jnp.where(at == w_other, 0.25, 0.0)
        col_weights.append(jnp.where(inside & (slot < z.half), weight, 0.0))
    span = z.coarse_rows * ROWS

    def one_row(r, carry):
        weight = jnp.where(h_main == r, 0.75, 0.0) + jnp.where(h_other == r, 0.25, 0.0)
        for half in range(2):
            at = pl.multiple_of(half * span + r * ROWS, ROWS)
            interp_ref[pl.ds(at, ROWS), :] = (col_weights[half] * weight).astype(BF16)
        return carry

    lax.fori_loop(0, z.coarse_rows, one_row, 0, unroll=z.coarse_rows <= 8)


def flatten_kernel(z, cot_ref, flat_ref, tall_ref, wide_ref):
    tall_ref[:, : z.width] = cot_ref[...].astype(F32).reshape(z.cout * z.height, z.width)
    wide_ref[...] = jnp.zeros(wide_ref.shape, F32)
    for h in range(z.height):
        piece = tall_ref[pl.ds(h, z.cout, stride=z.height), :]
        start = h * z.pitch + 2
        wide_ref[:, start : start + z.width] = piece[:, : z.width]
    flat_ref[...] = wide_ref[...].astype(BF16)


def backward(z, scale, flat_ref, ws_ref, row_ref, spread_ref):
    blend = row_ref[:, z.cout :]
    flat = flat_ref[...].astype(F32)
    d_skip = (flat * ((1.0 - blend) * scale)).astype(BF16)
    d_second = (flat * (blend * scale)).astype(BF16).astype(F32)
    d_second = jnp.concatenate([d_second, jnp.zeros((z.cout, z.wide - z.lanes), F32)], axis=1)
    back = []
    for p in range(3):
        for q in range(3):
            shift = (q - 1) * z.pitch + p - 1
            moved = d_second if shift == 0 else pltpu.roll(d_second, shift % z.wide, 1)
            k = (p * 3 + q) * z.cout
            spread_ref[k : k + z.cout, :] = moved[:, : z.lanes].astype(BF16)
            back.append(ws_ref[p, q])
    d_hidden = jnp.dot(
        jnp.concatenate(back, axis=1), spread_ref[...], preferred_element_type=F32
    )
    return d_skip, d_hidden


def prepare_kernel(
    z, scale, flat_ref, ws_ref, row_ref, d_hidden_ref, spread_ref, dskip_ref, interp_ref, bias_ref
):
    interpolation(z, interp_ref)
    diagonal = ints((z.cout, z.cout), 0) == ints((z.cout, z.cout), 1)
    bias_ref[...] = jnp.sum(jnp.where(diagonal, row_ref[:, : z.cout], 0.0), axis=1, keepdims=True)
    d_skip, d_hidden = backward(z, scale, flat_ref, ws_ref, row_ref, spread_ref)
    dskip_ref[...] = d_skip
    d_hidden_ref[...] = d_hidden


def holds_top(z):
    image, tile = lax.axis_index("img"), lax.axis_index("tile")
    bits = jnp.int32(0)
    for index, count in ((image, z.images), (tile, z.tiles)):
        k = 1
        while k < count:
            bits = bits ^ (lax.div(index, jnp.int32(k)) & 1)
            k *= 2
    return bits == 0


def gradients(z, d_hidden, d_skip, spread, slope, hidden, taps, centre):
    d_pre = (d_hidden * slope).astype(BF16)
    first = lax.dot_general(d_pre, taps, NT, preferred_element_type=F32)
    second = lax.dot_general(hidden, spread, NT, preferred_element_type=F32)
    skip = lax.dot_general(d_skip, centre, NT, preferred_element_type=F32)
    ones = jnp.ones((z.cout, z.lanes), BF16)
    biases = lax.dot_general(ones, d_pre, NT, preferred_element_type=F32)
    return jnp.concatenate([first, second, skip, biases], axis=1)


def forward_kernel(
    z, got_ref, d_hidden_ref, spread_ref, dskip_ref, wf_ref, bias_ref, interp_ref,
    sums_ref, up_ref, hidden_ref, other_taps_ref, other_hidden_ref, other_slope_ref, taps_ref,
):
    position = lax.axis_index("tile")
    n = ints((1, z.wide), 1) - 1
    w = n - (quotient(n + z.pitch, z.pitch) - 1) * z.pitch - 2
    m = ints((1, z.lanes), 1)
    mh = quotient(m, z.pitch)
    mw = m - mh * z.pitch - 2
    kernel = jnp.concatenate([wf_ref[p, q] for p in range(3) for q in range(3)], axis=1)
    for s, here_ref in enumerate((taps_ref, other_taps_ref)):
        tile = position ^ (s * z.pair)
        turned = got_ref[:, s * ROWS : (s + 1) * ROWS, :]
        turned = turned.reshape(z.coarse_rows * ROWS, 2 * z.cin).T
        windows = jnp.concatenate([turned[: z.cin], turned[z.cin :]], axis=1)
        up = jnp.dot(windows, interp_ref[...], preferred_element_type=F32)
        column = tile * z.width + w
        inside = jnp.where((column >= 0) & (column < z.width * z.tiles), 1.0, 0.0)
        up = (up * inside).astype(BF16).astype(F32)
        for p in range(3):
            for q in range(3):
                start = q * z.pitch + p
                moved = up if start == 0 else pltpu.roll(up, z.wide - start, 1)
                k = (p * 3 + q) * z.cin
                here_ref[k : k + z.cin, :] = moved[:, : z.lanes].astype(BF16)
        column = tile * z.width + mw
        inside = (mw >= -1) & (mw <= z.width) & (mh < z.height)
        inside = inside & (column >= 0) & (column < z.width * z.tiles)
        inside = jnp.where(inside, 1.0, 0.0)
        taps = here_ref[...]
        pre = jnp.dot(kernel, taps, preferred_element_type=F32) + bias_ref[...]
        sigma = 1.0 / (1.0 + jnp.exp(-pre))
        hidden = (pre * sigma * inside).astype(BF16)
        slope = sigma * (1.0 + pre * (1.0 - sigma)) * inside
        if s == 0:
            centre = here_ref[4 * z.cin : 5 * z.cin, :]
            up_ref[...] = centre
            hidden_ref[...] = hidden
            sums_ref[...] = gradients(
                z, d_hidden_ref[...], dskip_ref[...], spread_ref[...], slope, hidden, taps, centre
            )
        else:
            other_hidden_ref[...] = hidden
            other_slope_ref[...] = slope


def other_kernel(
    z, scale, sums_ref, taps_ref, hidden_ref, slope_ref, flat_ref, ws_ref, row_ref,
    keep_ref, give_ref, spread_ref,
):
    d_skip, d_hidden = backward(z, scale, flat_ref, ws_ref, row_ref, spread_ref)
    centre = taps_ref[4 * z.cin : 5 * z.cin, :]
    grads = sums_ref[...] + gradients(
        z, d_hidden, d_skip, spread_ref[...], slope_ref[...], hidden_ref[...], taps_ref[...], centre
    )
    full, used = keep_ref.shape[1], grads.shape[1]
    if full > used:
        grads = jnp.concatenate([grads, jnp.zeros((z.cout, full - used), F32)], axis=1)
    half = z.cout // 2
    top = holds_top(z)
    keep_ref[...] = jnp.where(top, grads[:half], grads[half:]).astype(BF16)
    give_ref[...] = jnp.where(top, grads[half:], grads[:half]).astype(BF16)


def blend_kernel(z, hidden_ref, up_ref, ws_ref, wk_ref, row_ref, out_ref, tall_ref):
    blend = row_ref[:, z.cout :]
    padded = jnp.concatenate(
        [hidden_ref[...].astype(F32), jnp.zeros((z.cout, z.wide - z.lanes), F32)], axis=1
    )
    padded = pltpu.roll(padded, z.pitch + 1, 1)
    taps = []
    for p in range(3):
        for q in range(3):
            start = q * z.pitch + p
            moved = padded if start == 0 else pltpu.roll(padded, z.wide - start, 1)
            taps.append(moved[:, : z.lanes].astype(BF16))
    taps = jnp.concatenate(taps, axis=0)
    kernel = ws_ref[...].reshape(9 * z.cout, z.cout).T
    second = jnp.dot(kernel, taps, preferred_element_type=F32)
    skip = jnp.dot(wk_ref[...], up_ref[...], preferred_element_type=F32)
    mixed = blend * second + (1.0 - blend) * skip
    for h in range(z.height):
        start = h * z.pitch + 2
        tall_ref[pl.ds(h, z.cout, stride=z.height), : z.width] = mixed[:, start : start + z.width]
    out_ref[...] = tall_ref[:, : z.width].reshape(out_ref.shape).astype(BF16)


def finish_kernel(z, mine_ref, other_ref, first_ref, bias_ref, second_ref, skip_ref):
    top = holds_top(z)
    mine, other = mine_ref[...], other_ref[...]
    total = jnp.concatenate(
        [jnp.where(top, mine, other), jnp.where(top, other, mine)], axis=0
    )
    at = 0
    for p in range(3):
        for q in range(3):
            first_ref[p, q] = total[:, at : at + z.cin]
            at += z.cin
    for p in range(3):
        for q in range(3):
            second_ref[p, q] = total[:, at : at + z.cout]
            at += z.cout
    skip_ref[...] = total[:, at : at + z.cin]
    at += z.cin
    bias_ref[...] = total[0:1, at : at + z.cout]


def call(body, outs, specs, scratch=(), flops=1000000):
    return pl.pallas_call(
        body,
        out_shape=outs,
        in_specs=specs,
        out_specs=jax.tree.map(lambda _: pl.BlockSpec(memory_space=pltpu.VMEM), outs),
        scratch_shapes=scratch,
        compiler_params=pltpu.CompilerParams(vmem_limit_bytes=48 * 1024 * 1024),
        cost_estimate=pl.CostEstimate(flops=flops, bytes_accessed=200000, transcendentals=0),
    )


def swap(values, images, tiles, across):
    a, b = across
    pairs = [
        (i * tiles + t, (i ^ a) * tiles + (t ^ b)) for i in range(images) for t in range(tiles)
    ]
    return lax.ppermute(values, ("img", "tile"), pairs)


def total_over_devices(keep, give, images, tiles):
    own = keep.astype(F32)
    if images >= 4:
        core = swap(give, images, tiles, (1, 0))
        cross = swap(keep, images, tiles, (3, 0))
        straight = swap(give, images, tiles, (2, 0))
        mine = (own + cross.astype(F32)) + (core.astype(F32) + straight.astype(F32))
    else:
        mine = own + swap(give, images, tiles, (1, 0)).astype(F32)
    bits = []
    k = 4
    while k < images:
        bits.append((k, 0))
        k *= 2
    k = 1
    while k < tiles // 2:
        bits.append((0, k))
        k *= 2
    odd = len(bits) % 2
    groups = [bits[:odd]] if odd else []
    groups += [(bits[at + 1], bits[at]) for at in range(odd, len(bits), 2)]
    for group in groups:
        sent = mine.astype(BF16)
        partners = [(a ^ 1, b) for a, b in group]
        if len(group) == 2:
            partners.append((group[0][0] ^ group[1][0], group[0][1] ^ group[1][1]))
        got = [swap(sent, images, tiles, across).astype(F32) for across in partners]
        mine = sent.astype(F32) + got[0]
        if len(got) == 3:
            mine = mine + (got[1] + got[2])
    return mine


def local(coarse, w_first, b_first, w_second, w_skip, fade_alpha, cotangent):
    tiles = lax.axis_size("tile")
    images = lax.axis_size("img")
    z = Sizes(coarse, cotangent, images, tiles)
    vmem = pl.BlockSpec(memory_space=pltpu.VMEM)
    bf, f32 = (lambda *s: jax.ShapeDtypeStruct(s, BF16)), (lambda *s: jax.ShapeDtypeStruct(s, F32))
    total_count = coarse.shape[0] * images * z.width * tiles * z.height
    scale = float(total_count) ** (-0.5)

    packed = call(
        functools.partial(pack_kernel, z), bf(tiles, 2 * ROWS, 2 * z.cin), [vmem]
    )(coarse.reshape(z.cin, z.coarse_cols))
    got = lax.all_to_all(packed, "tile", split_axis=0, concat_axis=0, tiled=True)

    flat = call(
        functools.partial(flatten_kernel, z),
        bf(z.cout, z.lanes),
        [vmem],
        [pltpu.VMEM((z.cout * z.height, 128), F32), pltpu.VMEM((z.cout, z.lanes), F32)],
    )(jnp.transpose(cotangent[0], (0, 2, 1)))
    other_flat = swap(flat, images, tiles, (0, z.pair))
    row = jnp.concatenate([b_first, fade_alpha]).reshape(1, z.cout + 1)
    d_hidden, spread, dskip, interp, bias = call(
        functools.partial(prepare_kernel, z, scale),
        (
            f32(z.cout, z.lanes),
            bf(9 * z.cout, z.lanes),
            bf(z.cout, z.lanes),
            bf(2 * z.coarse_rows * ROWS, z.wide),
            f32(z.cout, 1),
        ),
        [vmem] * 3,
    )(flat, w_second, row)

    used = 10 * z.cin + 10 * z.cout
    sums, up, hidden, *other = call(
        functools.partial(forward_kernel, z),
        (
            f32(z.cout, used),
            bf(z.cin, z.lanes),
            bf(z.cout, z.lanes),
            bf(9 * z.cin, z.lanes),
            bf(z.cout, z.lanes),
            f32(z.cout, z.lanes),
        ),
        [vmem] * 7,
        [pltpu.VMEM((9 * z.cin, z.lanes), BF16)],
    )(got, d_hidden, spread, dskip, jnp.transpose(w_first, (0, 1, 3, 2)), bias, interp)

    half = bf(z.cout // 2, up128(used))
    keep, give = call(
        functools.partial(other_kernel, z, scale),
        (half, half),
        [vmem] * 7,
        [pltpu.VMEM((9 * z.cout, z.lanes), BF16)],
    )(sums, *other, other_flat, w_second, row)

    blended = call(
        functools.partial(blend_kernel, z),
        bf(z.cout, z.height, z.width),
        [vmem] * 5,
        [pltpu.VMEM((z.cout * z.height, 128), F32)],
    )(hidden, up, w_second, jnp.transpose(w_skip), row)

    mine = total_over_devices(keep, give, images, tiles)
    mine, blended = lax.optimization_barrier((mine, blended))
    other = swap(mine, images, tiles, (1, 0))
    first, bias, second, skip = call(
        functools.partial(finish_kernel, z),
        (f32(3, 3, z.cout, z.cin), f32(1, z.cout), f32(3, 3, z.cout, z.cout), f32(z.cout, z.cin)),
        [vmem] * 2,
    )(mine, other)
    return (
        jnp.transpose(blended, (0, 2, 1))[None],
        jnp.transpose(first, (0, 1, 3, 2)),
        bias.reshape(z.cout),
        second,
        jnp.transpose(skip),
    )


def solution(mesh):
    placed = (P("img", None, "tile", None), P(), P(), P(), P(), P(), P("img", None, "tile", None))
    return jax.shard_map(
        local,
        mesh=mesh,
        in_specs=placed,
        out_specs=(P("img", None, "tile", None), P(), P(), P(), P()),
        check_vma=False,
    )
```

```python
import functools

import jax
import jax.numpy as jnp
from jax import lax
from jax.experimental import pallas as pl
from jax.experimental.pallas import tpu as pltpu
from jax.sharding import PartitionSpec as P

F32 = jnp.float32
BF16 = jnp.bfloat16
ROWS = 16
NT = (((1,), (1,)), ((), ()))


def up128(n):
    return -(-n // 128) * 128


def ints(shape, dim):
    return lax.broadcasted_iota(jnp.int32, shape, dim)


def quotient(values, divisor):
    return ((values.astype(F32) + 0.5) * (1.0 / divisor)).astype(jnp.int32)


class Sizes:
    def __init__(self, coarse, cotangent, images, tiles):
        self.images = images
        self.tiles = tiles
        self.cin = coarse.shape[1]
        self.cout = cotangent.shape[1]
        self.coarse_rows = coarse.shape[2] * tiles
        self.coarse_cols = coarse.shape[3]
        self.own_coarse = self.coarse_cols // tiles
        self.width = cotangent.shape[2]
        self.height = cotangent.shape[3]
        self.pitch = self.width + 4
        self.window = self.own_coarse + 4
        self.half = self.window // 2
        self.lanes = up128(self.height * self.pitch)
        self.pair = tiles // 2
        self.wide = up128(self.lanes + 2 * self.pitch + 2)


def pick_kernel(z, pick_ref):
    count = z.tiles * ROWS
    at = ints((count, z.coarse_cols), 0)
    col = ints((count, z.coarse_cols), 1)
    slot = lax.bitwise_and(at, ROWS - 1)
    want = lax.shift_right_logical(at, 4) * z.own_coarse - 2 + slot
    for half in range(2):
        here = jnp.clip(want + half * z.half, 0, z.coarse_cols - 1)
        pick_ref[half] = jnp.where((here == col) & (slot < z.half), 1.0, 0.0).astype(BF16)


def pack_kernel(z, coarse_ref, pick_ref, out_ref):
    row = coarse_ref[...]
    parts = [
        lax.dot_general(pick_ref[half], row, NT, preferred_element_type=F32) for half in range(2)
    ]
    packed = jnp.concatenate(parts, axis=1).astype(BF16).reshape(z.tiles, ROWS, 2 * z.cin)
    out_ref[:, :ROWS, :] = packed
    out_ref[: z.pair, ROWS:, :] = packed[z.pair :]
    out_ref[z.pair :, ROWS:, :] = packed[: z.pair]


def interpolation(z, interp_ref):
    n = ints((ROWS, z.wide), 1) - 1
    slot = ints((ROWS, z.wide), 0)
    h = quotient(n + z.pitch, z.pitch) - 2
    w = n - (h + 1) * z.pitch
    inside = (h >= 0) & (h < z.height)
    w_main = lax.shift_right_logical(w, 1) + 1
    w_other = w_main - 1 + 2 * lax.bitwise_and(w, 1)
    h_main = lax.shift_right_arithmetic(h, 1)
    h_other = jnp.clip(h_main - 1 + 2 * lax.bitwise_and(h, 1), 0, z.coarse_rows - 1)
    col_weights = []
    for half in range(2):
        at = slot + half * z.half
        weight = jnp.where(at == w_main, 0.75, 0.0) + jnp.where(at == w_other, 0.25, 0.0)
        col_weights.append(jnp.where(inside & (slot < z.half), weight, 0.0))
    span = z.coarse_rows * ROWS

    def one_row(r, carry):
        weight = jnp.where(h_main == r, 0.75, 0.0) + jnp.where(h_other == r, 0.25, 0.0)
        for half in range(2):
            at = pl.multiple_of(half * span + r * ROWS, ROWS)
            interp_ref[pl.ds(at, ROWS), :] = (col_weights[half] * weight).astype(BF16)
        return carry

    lax.fori_loop(0, z.coarse_rows, one_row, 0, unroll=z.coarse_rows <= 8)


def flatten_kernel(z, cot_ref, flat_ref, tall_ref, wide_ref):
    tall_ref[:, : z.width] = cot_ref[...].astype(F32).reshape(z.cout * z.height, z.width)
    wide_ref[...] = jnp.zeros(wide_ref.shape, F32)
    for h in range(z.height):
        piece = tall_ref[pl.ds(h, z.cout, stride=z.height), :]
        start = h * z.pitch + 2
        wide_ref[:, start : start + z.width] = piece[:, : z.width]
    flat_ref[...] = wide_ref[...].astype(BF16)


def backward(z, scale, flat_ref, ws_ref, row_ref, spread_ref):
    blend = row_ref[:, z.cout :]
    flat = flat_ref[...].astype(F32)
    d_skip = (flat * ((1.0 - blend) * scale)).astype(BF16)
    d_second = (flat * (blend * scale)).astype(BF16)
    d_second = jnp.concatenate([d_second, jnp.zeros((z.cout, z.wide - z.lanes), BF16)], axis=1)
    back = []
    for p in range(3):
        for q in range(3):
            shift = (q - 1) * z.pitch + p - 1
            moved = d_second if shift == 0 else pltpu.roll(d_second, shift % z.wide, 1)
            k = (p * 3 + q) * z.cout
            spread_ref[k : k + z.cout, :] = moved[:, : z.lanes]
            back.append(ws_ref[p, q])
    d_hidden = jnp.dot(
        jnp.concatenate(back, axis=1), spread_ref[...], preferred_element_type=F32
    )
    return d_skip, d_hidden


def prepare_kernel(
    z, scale, flat_ref, ws_ref, row_ref, d_hidden_ref, spread_ref, dskip_ref, interp_ref, bias_ref
):
    interpolation(z, interp_ref)
    diagonal = ints((z.cout, z.cout), 0) == ints((z.cout, z.cout), 1)
    bias_ref[...] = jnp.sum(jnp.where(diagonal, row_ref[:, : z.cout], 0.0), axis=1, keepdims=True)
    d_skip, d_hidden = backward(z, scale, flat_ref, ws_ref, row_ref, spread_ref)
    dskip_ref[...] = d_skip
    d_hidden_ref[...] = d_hidden


def holds_top(z):
    image, tile = lax.axis_index("img"), lax.axis_index("tile")
    bits = jnp.int32(0)
    for index, count in ((image, z.images), (tile, z.tiles)):
        k = 1
        while k < count:
            bits = bits ^ (lax.div(index, jnp.int32(k)) & 1)
            k *= 2
    return bits == 0


def gradients(z, d_hidden, d_skip, spread, slope, hidden, taps, centre):
    d_pre = (d_hidden * slope).astype(BF16)
    stacked = jnp.concatenate([d_pre, d_skip], axis=0)
    products = lax.dot_general(stacked, taps, NT, preferred_element_type=F32)
    first = products[: z.cout]
    skip = products[z.cout :, 4 * z.cin : 5 * z.cin]
    second = lax.dot_general(hidden, spread, NT, preferred_element_type=F32)
    ones = jnp.ones((z.cout, z.lanes), BF16)
    biases = lax.dot_general(ones, d_pre, NT, preferred_element_type=F32)
    return jnp.concatenate([first, second, skip, biases], axis=1)


def forward_kernel(
    z, got_ref, d_hidden_ref, spread_ref, dskip_ref, wf_ref, bias_ref, interp_ref,
    sums_ref, up_ref, hidden_ref, other_taps_ref, other_hidden_ref, other_slope_ref, taps_ref,
):
    position = lax.axis_index("tile")
    n = ints((1, z.wide), 1) - 1
    w = n - (quotient(n + z.pitch, z.pitch) - 1) * z.pitch - 2
    m = ints((1, z.lanes), 1)
    mh = quotient(m, z.pitch)
    mw = m - mh * z.pitch - 2
    kernel = jnp.concatenate([wf_ref[p, q] for p in range(3) for q in range(3)], axis=1)
    for s, here_ref in enumerate((taps_ref, other_taps_ref)):
        tile = position ^ (s * z.pair)
        turned = got_ref[:, s * ROWS : (s + 1) * ROWS, :]
        turned = turned.reshape(z.coarse_rows * ROWS, 2 * z.cin).T
        windows = jnp.concatenate([turned[: z.cin], turned[z.cin :]], axis=1)
        up = jnp.dot(windows, interp_ref[...], preferred_element_type=F32)
        column = tile * z.width + w
        inside = jnp.where((column >= 0) & (column < z.width * z.tiles), 1.0, 0.0)
        up = (up * inside).astype(BF16)
        for p in range(3):
            for q in range(3):
                start = q * z.pitch + p
                moved = up if start == 0 else pltpu.roll(up, z.wide - start, 1)
                k = (p * 3 + q) * z.cin
                here_ref[k : k + z.cin, :] = moved[:, : z.lanes]
        column = tile * z.width + mw
        inside = (mw >= -1) & (mw <= z.width) & (mh < z.height)
        inside = inside & (column >= 0) & (column < z.width * z.tiles)
        inside = jnp.where(inside, 1.0, 0.0)
        taps = here_ref[...]
        pre = jnp.dot(kernel, taps, preferred_element_type=F32) + bias_ref[...]
        sigma = 0.5 * jnp.tanh(0.5 * pre) + 0.5
        hidden = (pre * sigma * inside).astype(BF16)
        slope = sigma * (1.0 + pre * (1.0 - sigma)) * inside
        if s == 0:
            centre = here_ref[4 * z.cin : 5 * z.cin, :]
            up_ref[...] = centre
            hidden_ref[...] = hidden
            sums_ref[...] = gradients(
                z, d_hidden_ref[...], dskip_ref[...], spread_ref[...], slope, hidden, taps, centre
            )
        else:
            other_hidden_ref[...] = hidden
            other_slope_ref[...] = slope


def other_kernel(
    z, scale, sums_ref, taps_ref, hidden_ref, slope_ref, flat_ref, ws_ref, row_ref,
    keep_ref, give_ref, spread_ref,
):
    d_skip, d_hidden = backward(z, scale, flat_ref, ws_ref, row_ref, spread_ref)
    centre = taps_ref[4 * z.cin : 5 * z.cin, :]
    grads = sums_ref[...] + gradients(
        z, d_hidden, d_skip, spread_ref[...], slope_ref[...], hidden_ref[...], taps_ref[...], centre
    )
    full, used = keep_ref.shape[1], grads.shape[1]
    if full > used:
        grads = jnp.concatenate([grads, jnp.zeros((z.cout, full - used), F32)], axis=1)
    half = z.cout // 2
    top = holds_top(z)
    keep_ref[...] = jnp.where(top, grads[:half], grads[half:]).astype(BF16)
    give_ref[...] = jnp.where(top, grads[half:], grads[:half]).astype(BF16)


def blend_kernel(z, hidden_ref, up_ref, ws_ref, wk_ref, row_ref, out_ref, tall_ref):
    blend = row_ref[:, z.cout :]
    padded = jnp.concatenate(
        [hidden_ref[...].astype(F32), jnp.zeros((z.cout, z.wide - z.lanes), F32)], axis=1
    )
    padded = pltpu.roll(padded, z.pitch + 1, 1)
    taps = []
    for p in range(3):
        for q in range(3):
            start = q * z.pitch + p
            moved = padded if start == 0 else pltpu.roll(padded, z.wide - start, 1)
            taps.append(moved[:, : z.lanes].astype(BF16))
    taps = jnp.concatenate(taps, axis=0)
    kernel = ws_ref[...].reshape(9 * z.cout, z.cout).T
    second = jnp.dot(kernel, taps, preferred_element_type=F32)
    skip = jnp.dot(wk_ref[...], up_ref[...], preferred_element_type=F32)
    mixed = blend * second + (1.0 - blend) * skip
    for h in range(z.height):
        start = h * z.pitch + 2
        tall_ref[pl.ds(h, z.cout, stride=z.height), : z.width] = mixed[:, start : start + z.width]
    out_ref[...] = tall_ref[:, : z.width].reshape(out_ref.shape).astype(BF16)


def finish_kernel(z, mine_ref, other_ref, first_ref, bias_ref, second_ref, skip_ref):
    top = holds_top(z)
    mine, other = mine_ref[...], other_ref[...]
    total = jnp.concatenate(
        [jnp.where(top, mine, other), jnp.where(top, other, mine)], axis=0
    )
    at = 0
    for p in range(3):
        for q in range(3):
            first_ref[p, q] = total[:, at : at + z.cin]
            at += z.cin
    for p in range(3):
        for q in range(3):
            second_ref[p, q] = total[:, at : at + z.cout]
            at += z.cout
    skip_ref[...] = total[:, at : at + z.cin]
    at += z.cin
    bias_ref[...] = total[0:1, at : at + z.cout]


def call(body, outs, specs, scratch=(), flops=1000000):
    return pl.pallas_call(
        body,
        out_shape=outs,
        in_specs=specs,
        out_specs=jax.tree.map(lambda _: pl.BlockSpec(memory_space=pltpu.VMEM), outs),
        scratch_shapes=scratch,
        compiler_params=pltpu.CompilerParams(vmem_limit_bytes=48 * 1024 * 1024),
        cost_estimate=pl.CostEstimate(flops=flops, bytes_accessed=200000, transcendentals=0),
    )


def swap(values, images, tiles, across):
    a, b = across
    pairs = [
        (i * tiles + t, (i ^ a) * tiles + (t ^ b)) for i in range(images) for t in range(tiles)
    ]
    return lax.ppermute(values, ("img", "tile"), pairs)


def total_over_devices(keep, give, images, tiles):
    own = keep.astype(F32)
    if images >= 4:
        core = swap(give, images, tiles, (1, 0))
        cross = swap(keep, images, tiles, (3, 0))
        straight = swap(give, images, tiles, (2, 0))
        mine = (own + cross.astype(F32)) + (core.astype(F32) + straight.astype(F32))
    else:
        mine = own + swap(give, images, tiles, (1, 0)).astype(F32)
    bits = []
    k = 4
    while k < images:
        bits.append((k, 0))
        k *= 2
    k = 1
    while k < tiles // 2:
        bits.append((0, k))
        k *= 2
    odd = len(bits) % 2
    groups = [bits[:odd]] if odd else []
    groups += [(bits[at + 1], bits[at]) for at in range(odd, len(bits), 2)]
    for group in groups:
        sent = mine.astype(BF16)
        partners = [(a ^ 1, b) for a, b in group]
        if len(group) == 2:
            partners.append((group[0][0] ^ group[1][0], group[0][1] ^ group[1][1]))
        got = [swap(sent, images, tiles, across).astype(F32) for across in partners]
        mine = sent.astype(F32) + got[0]
        if len(got) == 3:
            mine = mine + (got[1] + got[2])
    return mine


def local(coarse, w_first, b_first, w_second, w_skip, fade_alpha, cotangent):
    tiles = lax.axis_size("tile")
    images = lax.axis_size("img")
    z = Sizes(coarse, cotangent, images, tiles)
    vmem = pl.BlockSpec(memory_space=pltpu.VMEM)
    bf, f32 = (lambda *s: jax.ShapeDtypeStruct(s, BF16)), (lambda *s: jax.ShapeDtypeStruct(s, F32))
    total_count = coarse.shape[0] * images * z.width * tiles * z.height
    scale = float(total_count) ** (-0.5)

    picks = call(functools.partial(pick_kernel, z), bf(2, tiles * ROWS, z.coarse_cols), [])()
    packed = call(
        functools.partial(pack_kernel, z), bf(tiles, 2 * ROWS, 2 * z.cin), [vmem] * 2
    )(coarse.reshape(z.cin, z.coarse_cols), picks)
    got = lax.all_to_all(packed, "tile", split_axis=0, concat_axis=0, tiled=True)

    flat = call(
        functools.partial(flatten_kernel, z),
        bf(z.cout, z.lanes),
        [vmem],
        [pltpu.VMEM((z.cout * z.height, 128), F32), pltpu.VMEM((z.cout, z.lanes), F32)],
    )(jnp.transpose(cotangent[0], (0, 2, 1)))
    other_flat = swap(flat, images, tiles, (0, z.pair))
    row = jnp.concatenate([b_first, fade_alpha]).reshape(1, z.cout + 1)
    d_hidden, spread, dskip, interp, bias = call(
        functools.partial(prepare_kernel, z, scale),
        (
            f32(z.cout, z.lanes),
            bf(9 * z.cout, z.lanes),
            bf(z.cout, z.lanes),
            bf(2 * z.coarse_rows * ROWS, z.wide),
            f32(z.cout, 1),
        ),
        [vmem] * 3,
    )(flat, w_second, row)

    used = 10 * z.cin + 10 * z.cout
    sums, up, hidden, *other = call(
        functools.partial(forward_kernel, z),
        (
            f32(z.cout, used),
            bf(z.cin, z.lanes),
            bf(z.cout, z.lanes),
            bf(9 * z.cin, z.lanes),
            bf(z.cout, z.lanes),
            f32(z.cout, z.lanes),
        ),
        [vmem] * 7,
        [pltpu.VMEM((9 * z.cin, z.lanes), BF16)],
    )(got, d_hidden, spread, dskip, jnp.transpose(w_first, (0, 1, 3, 2)), bias, interp)

    half = bf(z.cout // 2, up128(used))
    keep, give = call(
        functools.partial(other_kernel, z, scale),
        (half, half),
        [vmem] * 7,
        [pltpu.VMEM((9 * z.cout, z.lanes), BF16)],
    )(sums, *other, other_flat, w_second, row)

    blended = call(
        functools.partial(blend_kernel, z),
        bf(z.cout, z.height, z.width),
        [vmem] * 5,
        [pltpu.VMEM((z.cout * z.height, 128), F32)],
    )(hidden, up, w_second, jnp.transpose(w_skip), row)

    mine = total_over_devices(keep, give, images, tiles)
    mine, blended = lax.optimization_barrier((mine, blended))
    other = swap(mine, images, tiles, (1, 0))
    first, bias, second, skip = call(
        functools.partial(finish_kernel, z),
        (f32(3, 3, z.cout, z.cin), f32(1, z.cout), f32(3, 3, z.cout, z.cout), f32(z.cout, z.cin)),
        [vmem] * 2,
    )(mine, other)
    return (
        jnp.transpose(blended, (0, 2, 1))[None],
        jnp.transpose(first, (0, 1, 3, 2)),
        bias.reshape(z.cout),
        second,
        jnp.transpose(skip),
    )


def solution(mesh):
    placed = (P("img", None, "tile", None), P(), P(), P(), P(), P(), P("img", None, "tile", None))
    return jax.shard_map(
        local,
        mesh=mesh,
        in_specs=placed,
        out_specs=(P("img", None, "tile", None), P(), P(), P(), P()),
        check_vma=False,
    )
```

```python
import functools

import jax
import jax.numpy as jnp
from jax import lax
from jax.experimental import pallas as pl
from jax.experimental.pallas import tpu as pltpu
from jax.sharding import PartitionSpec as P

F32 = jnp.float32
BF16 = jnp.bfloat16
ROWS = 16
NT = (((1,), (1,)), ((), ()))


def up128(n):
    return -(-n // 128) * 128


def ints(shape, dim):
    return lax.broadcasted_iota(jnp.int32, shape, dim)


def quotient(values, divisor):
    return ((values.astype(F32) + 0.5) * (1.0 / divisor)).astype(jnp.int32)


class Sizes:
    def __init__(self, coarse, cotangent, images, tiles):
        self.images = images
        self.tiles = tiles
        self.cin = coarse.shape[1]
        self.cout = cotangent.shape[1]
        self.coarse_rows = coarse.shape[2] * tiles
        self.coarse_cols = coarse.shape[3]
        self.own_coarse = self.coarse_cols // tiles
        self.width = cotangent.shape[2]
        self.height = cotangent.shape[3]
        self.pitch = self.width + 4
        self.window = self.own_coarse + 4
        self.half = self.window // 2
        self.lanes = up128(self.height * self.pitch)
        self.pair = tiles // 2
        self.wide = up128(self.lanes + 2 * self.pitch + 2)


def pick_kernel(z, pick_ref):
    count = z.tiles * ROWS
    at = ints((count, z.coarse_cols), 0)
    col = ints((count, z.coarse_cols), 1)
    slot = lax.bitwise_and(at, ROWS - 1)
    want = lax.shift_right_logical(at, 4) * z.own_coarse - 2 + slot
    for half in range(2):
        here = jnp.clip(want + half * z.half, 0, z.coarse_cols - 1)
        pick_ref[half] = jnp.where((here == col) & (slot < z.half), 1.0, 0.0).astype(BF16)


def pack_kernel(z, coarse_ref, pick_ref, out_ref):
    row = coarse_ref[...]
    parts = [
        lax.dot_general(pick_ref[half], row, NT, preferred_element_type=F32) for half in range(2)
    ]
    packed = jnp.concatenate(parts, axis=1).astype(BF16).reshape(z.tiles, ROWS, 2 * z.cin)
    out_ref[:, :ROWS, :] = packed
    out_ref[: z.pair, ROWS:, :] = packed[z.pair :]
    out_ref[z.pair :, ROWS:, :] = packed[: z.pair]


def interpolation(z, interp_ref):
    n = ints((ROWS, z.wide), 1) - 1
    slot = ints((ROWS, z.wide), 0)
    h = quotient(n + z.pitch, z.pitch) - 2
    w = n - (h + 1) * z.pitch
    inside = (h >= 0) & (h < z.height)
    w_main = lax.shift_right_logical(w, 1) + 1
    w_other = w_main - 1 + 2 * lax.bitwise_and(w, 1)
    h_main = lax.shift_right_arithmetic(h, 1)
    h_other = jnp.clip(h_main - 1 + 2 * lax.bitwise_and(h, 1), 0, z.coarse_rows - 1)
    col_weights = []
    for half in range(2):
        at = slot + half * z.half
        weight = jnp.where(at == w_main, 0.75, 0.0) + jnp.where(at == w_other, 0.25, 0.0)
        col_weights.append(jnp.where(inside & (slot < z.half), weight, 0.0))
    span = z.coarse_rows * ROWS

    def one_row(r, carry):
        weight = jnp.where(h_main == r, 0.75, 0.0) + jnp.where(h_other == r, 0.25, 0.0)
        for half in range(2):
            at = pl.multiple_of(half * span + r * ROWS, ROWS)
            interp_ref[pl.ds(at, ROWS), :] = (col_weights[half] * weight).astype(BF16)
        return carry

    lax.fori_loop(0, z.coarse_rows, one_row, 0, unroll=z.coarse_rows <= 8)


def flatten_kernel(z, cot_ref, flat_ref, tall_ref, wide_ref):
    tall_ref[:, : z.width] = cot_ref[...].astype(F32).reshape(z.cout * z.height, z.width)
    wide_ref[...] = jnp.zeros(wide_ref.shape, F32)
    for h in range(z.height):
        piece = tall_ref[pl.ds(h, z.cout, stride=z.height), :]
        start = h * z.pitch + 2
        wide_ref[:, start : start + z.width] = piece[:, : z.width]
    flat_ref[...] = wide_ref[...].astype(BF16)


def backward(z, scale, flat_ref, ws_ref, row_ref, spread_ref):
    blend = row_ref[:, z.cout :]
    flat = flat_ref[...].astype(F32)
    d_skip = (flat * ((1.0 - blend) * scale)).astype(BF16)
    d_second = (flat * (blend * scale)).astype(BF16)
    d_second = jnp.concatenate([d_second, jnp.zeros((z.cout, z.wide - z.lanes), BF16)], axis=1)
    back = []
    for p in range(3):
        for q in range(3):
            shift = (q - 1) * z.pitch + p - 1
            moved = d_second if shift == 0 else pltpu.roll(d_second, shift % z.wide, 1)
            k = (p * 3 + q) * z.cout
            spread_ref[k : k + z.cout, :] = moved[:, : z.lanes]
            back.append(ws_ref[p, q])
    d_hidden = jnp.dot(
        jnp.concatenate(back, axis=1), spread_ref[...], preferred_element_type=F32
    )
    return d_skip, d_hidden


def prepare_kernel(
    z, scale, flat_ref, ws_ref, row_ref, d_hidden_ref, spread_ref, dskip_ref, interp_ref, bias_ref
):
    interpolation(z, interp_ref)
    diagonal = ints((z.cout, z.cout), 0) == ints((z.cout, z.cout), 1)
    bias_ref[...] = jnp.sum(jnp.where(diagonal, row_ref[:, : z.cout], 0.0), axis=1, keepdims=True)
    d_skip, d_hidden = backward(z, scale, flat_ref, ws_ref, row_ref, spread_ref)
    dskip_ref[...] = d_skip
    d_hidden_ref[...] = d_hidden


def holds_top(z):
    image, tile = lax.axis_index("img"), lax.axis_index("tile")
    bits = jnp.int32(0)
    for index, count in ((image, z.images), (tile, z.tiles)):
        k = 1
        while k < count:
            bits = bits ^ (lax.div(index, jnp.int32(k)) & 1)
            k *= 2
    return bits == 0


def gradients(z, d_hidden, d_skip, spread, slope, hidden, taps, centre):
    d_pre = (d_hidden * slope).astype(BF16)
    stacked = jnp.concatenate([d_pre, d_skip], axis=0)
    products = lax.dot_general(stacked, taps, NT, preferred_element_type=F32)
    first = products[: z.cout]
    skip = products[z.cout :, 4 * z.cin : 5 * z.cin]
    second = lax.dot_general(hidden, spread, NT, preferred_element_type=F32)
    ones = jnp.ones((z.cout, z.lanes), BF16)
    biases = lax.dot_general(ones, d_pre, NT, preferred_element_type=F32)
    return jnp.concatenate([first, second, skip, biases], axis=1)


def forward_kernel(
    z, got_ref, d_hidden_ref, spread_ref, dskip_ref, wf_ref, bias_ref, interp_ref,
    sums_ref, up_ref, hidden_ref, other_taps_ref, other_hidden_ref, other_slope_ref, taps_ref,
):
    position = lax.axis_index("tile")
    n = ints((1, z.wide), 1) - 1
    w = n - (quotient(n + z.pitch, z.pitch) - 1) * z.pitch - 2
    m = ints((1, z.lanes), 1)
    mh = quotient(m, z.pitch)
    mw = m - mh * z.pitch - 2
    kernel = jnp.concatenate([wf_ref[p, q] for p in range(3) for q in range(3)], axis=1)
    for s, here_ref in enumerate((taps_ref, other_taps_ref)):
        tile = position ^ (s * z.pair)
        turned = got_ref[:, s * ROWS : (s + 1) * ROWS, :]
        turned = turned.reshape(z.coarse_rows * ROWS, 2 * z.cin).T
        windows = jnp.concatenate([turned[: z.cin], turned[z.cin :]], axis=1)
        up = jnp.dot(windows, interp_ref[...], preferred_element_type=F32)
        column = tile * z.width + w
        inside = jnp.where((column >= 0) & (column < z.width * z.tiles), 1.0, 0.0)
        up = (up * inside).astype(BF16)
        for p in range(3):
            for q in range(3):
                start = q * z.pitch + p
                moved = up if start == 0 else pltpu.roll(up, z.wide - start, 1)
                k = (p * 3 + q) * z.cin
                here_ref[k : k + z.cin, :] = moved[:, : z.lanes]
        column = tile * z.width + mw
        inside = (mw >= -1) & (mw <= z.width) & (mh < z.height)
        inside = inside & (column >= 0) & (column < z.width * z.tiles)
        inside = jnp.where(inside, 1.0, 0.0)
        taps = here_ref[...]
        pre = jnp.dot(kernel, taps, preferred_element_type=F32) + bias_ref[...]
        sigma = 0.5 * jnp.tanh(0.5 * pre) + 0.5
        hidden = (pre * sigma * inside).astype(BF16)
        slope = sigma * (1.0 + pre * (1.0 - sigma)) * inside
        if s == 0:
            centre = here_ref[4 * z.cin : 5 * z.cin, :]
            up_ref[...] = centre
            hidden_ref[...] = hidden
            sums_ref[...] = gradients(
                z, d_hidden_ref[...], dskip_ref[...], spread_ref[...], slope, hidden, taps, centre
            )
        else:
            other_hidden_ref[...] = hidden
            other_slope_ref[...] = slope


def other_kernel(
    z, scale, sums_ref, taps_ref, hidden_ref, slope_ref, flat_ref, ws_ref, row_ref,
    keep_ref, give_ref, spread_ref,
):
    d_skip, d_hidden = backward(z, scale, flat_ref, ws_ref, row_ref, spread_ref)
    centre = taps_ref[4 * z.cin : 5 * z.cin, :]
    grads = sums_ref[...] + gradients(
        z, d_hidden, d_skip, spread_ref[...], slope_ref[...], hidden_ref[...], taps_ref[...], centre
    )
    full, used = keep_ref.shape[1], grads.shape[1]
    if full > used:
        grads = jnp.concatenate([grads, jnp.zeros((z.cout, full - used), F32)], axis=1)
    half = z.cout // 2
    top = holds_top(z)
    keep_ref[...] = jnp.where(top, grads[:half], grads[half:]).astype(BF16)
    give_ref[...] = jnp.where(top, grads[half:], grads[:half]).astype(BF16)


def blend_kernel(z, hidden_ref, up_ref, ws_ref, wk_ref, row_ref, out_ref, tall_ref):
    blend = row_ref[:, z.cout :]
    padded = jnp.concatenate(
        [hidden_ref[...].astype(F32), jnp.zeros((z.cout, z.wide - z.lanes), F32)], axis=1
    )
    padded = pltpu.roll(padded, z.pitch + 1, 1)
    taps = []
    for p in range(3):
        for q in range(3):
            start = q * z.pitch + p
            moved = padded if start == 0 else pltpu.roll(padded, z.wide - start, 1)
            taps.append(moved[:, : z.lanes].astype(BF16))
    taps = jnp.concatenate(taps, axis=0)
    kernel = ws_ref[...].reshape(9 * z.cout, z.cout).T
    second = jnp.dot(kernel, taps, preferred_element_type=F32)
    skip = jnp.dot(wk_ref[...], up_ref[...], preferred_element_type=F32)
    mixed = blend * second + (1.0 - blend) * skip
    for h in range(z.height):
        start = h * z.pitch + 2
        tall_ref[pl.ds(h, z.cout, stride=z.height), : z.width] = mixed[:, start : start + z.width]
    out_ref[...] = tall_ref[:, : z.width].reshape(out_ref.shape).astype(BF16)


def finish_kernel(z, mine_ref, other_ref, first_ref, bias_ref, second_ref, skip_ref):
    top = holds_top(z)
    mine, other = mine_ref[...].astype(F32), other_ref[...].astype(F32)
    total = jnp.concatenate(
        [jnp.where(top, mine, other), jnp.where(top, other, mine)], axis=0
    )
    at = 0
    for p in range(3):
        for q in range(3):
            first_ref[p, q] = total[:, at : at + z.cin]
            at += z.cin
    for p in range(3):
        for q in range(3):
            second_ref[p, q] = total[:, at : at + z.cout]
            at += z.cout
    skip_ref[...] = total[:, at : at + z.cin]
    at += z.cin
    bias_ref[...] = total[0:1, at : at + z.cout]


def call(body, outs, specs, scratch=(), flops=1000000):
    return pl.pallas_call(
        body,
        out_shape=outs,
        in_specs=specs,
        out_specs=jax.tree.map(lambda _: pl.BlockSpec(memory_space=pltpu.VMEM), outs),
        scratch_shapes=scratch,
        compiler_params=pltpu.CompilerParams(vmem_limit_bytes=48 * 1024 * 1024),
        cost_estimate=pl.CostEstimate(flops=flops, bytes_accessed=200000, transcendentals=0),
    )


def swap(values, images, tiles, across):
    a, b = across
    pairs = [
        (i * tiles + t, (i ^ a) * tiles + (t ^ b)) for i in range(images) for t in range(tiles)
    ]
    return lax.ppermute(values, ("img", "tile"), pairs)


def total_over_devices(keep, give, images, tiles):
    own = keep.astype(F32)
    if images >= 4:
        core = swap(give, images, tiles, (1, 0))
        cross = swap(keep, images, tiles, (3, 0))
        straight = swap(give, images, tiles, (2, 0))
        mine = (own + cross.astype(F32)) + (core.astype(F32) + straight.astype(F32))
    else:
        mine = own + swap(give, images, tiles, (1, 0)).astype(F32)
    bits = []
    k = 4
    while k < images:
        bits.append((k, 0))
        k *= 2
    k = 1
    while k < tiles // 2:
        bits.append((0, k))
        k *= 2
    odd = len(bits) % 2
    groups = [bits[:odd]] if odd else []
    groups += [(bits[at + 1], bits[at]) for at in range(odd, len(bits), 2)]
    for group in groups:
        sent = mine.astype(BF16)
        partners = [(a ^ 1, b) for a, b in group]
        if len(group) == 2:
            partners.append((group[0][0] ^ group[1][0], group[0][1] ^ group[1][1]))
        got = [swap(sent, images, tiles, across).astype(F32) for across in partners]
        mine = sent.astype(F32) + got[0]
        if len(got) == 3:
            mine = mine + (got[1] + got[2])
    return mine


def local(coarse, w_first, b_first, w_second, w_skip, fade_alpha, cotangent):
    tiles = lax.axis_size("tile")
    images = lax.axis_size("img")
    z = Sizes(coarse, cotangent, images, tiles)
    vmem = pl.BlockSpec(memory_space=pltpu.VMEM)
    bf, f32 = (lambda *s: jax.ShapeDtypeStruct(s, BF16)), (lambda *s: jax.ShapeDtypeStruct(s, F32))
    total_count = coarse.shape[0] * images * z.width * tiles * z.height
    scale = float(total_count) ** (-0.5)

    picks = call(functools.partial(pick_kernel, z), bf(2, tiles * ROWS, z.coarse_cols), [])()
    packed = call(
        functools.partial(pack_kernel, z), bf(tiles, 2 * ROWS, 2 * z.cin), [vmem] * 2
    )(coarse.reshape(z.cin, z.coarse_cols), picks)
    got = lax.all_to_all(packed, "tile", split_axis=0, concat_axis=0, tiled=True)

    flat = call(
        functools.partial(flatten_kernel, z),
        bf(z.cout, z.lanes),
        [vmem],
        [pltpu.VMEM((z.cout * z.height, 128), F32), pltpu.VMEM((z.cout, z.lanes), F32)],
    )(jnp.transpose(cotangent[0], (0, 2, 1)))
    other_flat = swap(flat, images, tiles, (0, z.pair))
    row = jnp.concatenate([b_first, fade_alpha]).reshape(1, z.cout + 1)
    d_hidden, spread, dskip, interp, bias = call(
        functools.partial(prepare_kernel, z, scale),
        (
            f32(z.cout, z.lanes),
            bf(9 * z.cout, z.lanes),
            bf(z.cout, z.lanes),
            bf(2 * z.coarse_rows * ROWS, z.wide),
            f32(z.cout, 1),
        ),
        [vmem] * 3,
    )(flat, w_second, row)

    used = 10 * z.cin + 10 * z.cout
    sums, up, hidden, *other = call(
        functools.partial(forward_kernel, z),
        (
            f32(z.cout, used),
            bf(z.cin, z.lanes),
            bf(z.cout, z.lanes),
            bf(9 * z.cin, z.lanes),
            bf(z.cout, z.lanes),
            f32(z.cout, z.lanes),
        ),
        [vmem] * 7,
        [pltpu.VMEM((9 * z.cin, z.lanes), BF16)],
    )(got, d_hidden, spread, dskip, jnp.transpose(w_first, (0, 1, 3, 2)), bias, interp)

    half = bf(z.cout // 2, up128(used))
    keep, give = call(
        functools.partial(other_kernel, z, scale),
        (half, half),
        [vmem] * 7,
        [pltpu.VMEM((9 * z.cout, z.lanes), BF16)],
    )(sums, *other, other_flat, w_second, row)

    blended = call(
        functools.partial(blend_kernel, z),
        bf(z.cout, z.height, z.width),
        [vmem] * 5,
        [pltpu.VMEM((z.cout * z.height, 128), F32)],
    )(hidden, up, w_second, jnp.transpose(w_skip), row)

    mine = total_over_devices(keep, give, images, tiles)
    mine, blended = lax.optimization_barrier((mine, blended))
    mine = mine.astype(BF16)
    other = swap(mine, images, tiles, (1, 0))
    first, bias, second, skip = call(
        functools.partial(finish_kernel, z),
        (f32(3, 3, z.cout, z.cin), f32(1, z.cout), f32(3, 3, z.cout, z.cout), f32(z.cout, z.cin)),
        [vmem] * 2,
    )(mine, other)
    return (
        jnp.transpose(blended, (0, 2, 1))[None],
        jnp.transpose(first, (0, 1, 3, 2)),
        bias.reshape(z.cout),
        second,
        jnp.transpose(skip),
    )


def solution(mesh):
    placed = (P("img", None, "tile", None), P(), P(), P(), P(), P(), P("img", None, "tile", None))
    return jax.shard_map(
        local,
        mesh=mesh,
        in_specs=placed,
        out_specs=(P("img", None, "tile", None), P(), P(), P(), P()),
        check_vma=False,
    )
```
